256 devices in a mesh: dp: 16 (over y_hi, z), tensor: 16 (over y_lo, x, core).
Axes of the slice: x: 4, y: 4 (y_hi: 2, y_lo: 2; y = y_hi * 2 + y_lo), z: 8, core: 2. Of those that a mesh axis runs over, the one named last changes fastest.
Arguments:
- patches: bfloat16 [32768, 4096], P(('dp', 'tensor')), may hold values from -8 to 8
- cotangent: bfloat16 [32768, 4096], P(('dp', 'tensor')), may hold values from -40 to 40
- preact: bfloat16 [32768, 12288], P('dp', 'tensor'), may hold values from -8 to 8
- down_matrix: bfloat16 [12288, 4096], P('tensor', 'dp'), may hold values from -0.0546875 to 0.0546875
- up_adapter_first: bfloat16 [32, 4096], replicated, may hold values from -0.09375 to 0.09375
- up_adapter_second: bfloat16 [32, 12288], P(None, 'tensor'), may hold values from -0.0546875 to 0.0546875
- down_adapter_first: bfloat16 [32, 12288], P(None, 'tensor'), may hold values from -0.0546875 to 0.0546875
- down_adapter_second: bfloat16 [32, 4096], replicated, may hold values from -0.09375 to 0.09375
Outputs:
- preact_gradient: bfloat16 [32768, 12288], P('dp', 'tensor')
- grad_a1: float32 [32, 4096], P(None, 'tensor')
- grad_b1: float32 [32, 12288], P(None, 'tensor')
- grad_a2: float32 [32, 12288], P(None, 'tensor')
- grad_b2: float32 [32, 4096], P(None, 'tensor')
The draws below stay inside these ranges and needn't reach their ends.
All inputs are finite; a program needn't handle non-finite values.
Results may differ from the reference program's by a relative error of at most 0.0051.
Values may be sent and summed in bfloat16 or wider, within the bound.
No kernel may reach another device: no remote copies, remote signals or barrier semaphores. Data moves between devices by JAX's collectives and lax.ppermute only.
A program may use at most 128 MiB of HBM per device.

```python
import math
import jax
import jax.numpy as jnp
from jax import lax

MODEL_FEATS = 4096
HIDDEN_UNITS = 12288
ADAPTER_RANK = 32
PATCHES = 256
IMAGES = 128
TOKENS = 32768


def column_scale(key, entries):
    position = jnp.arange(entries).astype(jnp.float32) / (entries - 1)
    roughness = jax.random.uniform(key, (entries,), jnp.float32, 0.7, 1.4)
    return 0.6 * jnp.exp(position * jnp.log(3.0)) * roughness


def draw_patches(key, part):
    key = jax.random.fold_in(key, 11)
    scale_key, value_key = jax.random.split(key, 2)
    col_scale = column_scale(scale_key, MODEL_FEATS)
    values = jax.random.normal(value_key, (TOKENS, MODEL_FEATS), jnp.float32) * col_scale
    return jnp.clip(values, -8.0, 8.0).astype(jnp.bfloat16)


def draw_cotangent(key, part):
    key = jax.random.fold_in(key, 23)
    scale_key, image_key, value_key = jax.random.split(key, 3)
    col_scale = column_scale(scale_key, MODEL_FEATS)
    image_scale = jnp.exp(jax.random.uniform(image_key, (IMAGES,), jnp.float32, jnp.log(0.25), jnp.log(4.0)))
    row_scale = image_scale[jnp.arange(TOKENS) // PATCHES][:, None]
    values = jax.random.normal(value_key, (TOKENS, MODEL_FEATS), jnp.float32) * col_scale
    return jnp.clip(values * row_scale, -40.0, 40.0).astype(jnp.bfloat16)


def draw_preact(key, part):
    key = jax.random.fold_in(key, 37)
    scale_key, value_key = jax.random.split(key, 2)
    col_scale = column_scale(scale_key, HIDDEN_UNITS)
    values = jax.random.normal(value_key, (TOKENS, HIDDEN_UNITS), jnp.float32) * col_scale
    return jnp.clip(values, -8.0, 8.0).astype(jnp.bfloat16)


def steps_of(rng, extent, cuts, least, top_value):
    def one(dim, blocks):
        draws = jax.random.uniform(jax.random.fold_in(jax.random.fold_in(rng, 6), dim), (blocks,), jnp.float32, least / len(cuts), top_value / len(cuts))
        return jnp.repeat(jnp.exp(draws), extent[dim] // blocks).reshape((-1,) + (1,) * (len(extent) - dim - 1))

    level = one(*cuts[0])
    for cut in cuts[1:]:
        level = level * one(*cut)
    return level


def bell_draw(rng, shape, spread, most, cuts=(), held_as=jnp.bfloat16):
    drawn = jax.random.normal(rng, shape, jnp.float32) * spread
    if len(cuts) > 0:
        drawn = steps_of(rng, shape, cuts, -0.22, 0.18) * drawn
    return jnp.clip(drawn, min=-most, max=most).astype(held_as)


def setup_inputs(seed: int = 0) -> dict:
    splits = jax.random.split(jax.random.key(seed), 9)
    patches = draw_patches(jax.random.fold_in(splits[8], 71), 0)
    cotangent = draw_cotangent(jax.random.fold_in(splits[8], 71), 0)
    preact = draw_preact(jax.random.fold_in(splits[8], 71), 0)
    down_matrix = bell_draw(splits[3], (HIDDEN_UNITS, MODEL_FEATS), HIDDEN_UNITS ** -0.5, 0.0546875, ((0, 16), (1, 16)))
    up_adapter_first = bell_draw(splits[4], (ADAPTER_RANK, MODEL_FEATS), MODEL_FEATS ** -0.5, 0.09375)
    up_adapter_second = bell_draw(splits[5], (ADAPTER_RANK, HIDDEN_UNITS), HIDDEN_UNITS ** -0.5, 0.0546875, ((1, 16),))
    down_adapter_first = bell_draw(splits[6], (ADAPTER_RANK, HIDDEN_UNITS), HIDDEN_UNITS ** -0.5, 0.0546875, ((1, 16),))
    down_adapter_second = bell_draw(splits[7], (ADAPTER_RANK, MODEL_FEATS), MODEL_FEATS ** -0.5, 0.09375)
    return {"patches": patches, "cotangent": cotangent, "preact": preact, "down_matrix": down_matrix, "up_adapter_first": up_adapter_first, "up_adapter_second": up_adapter_second, "down_adapter_first": down_adapter_first, "down_adapter_second": down_adapter_second}


clip_scale = 0.02
norm_eps = 1e-06

def contract_trailing(left_side, right_side):
    return lax.dot_general(left_side, right_side, (((1,), (1,)), ((), ())), preferred_element_type=jnp.float32)

def contract_first(left_side, right_side):
    return lax.dot_general(left_side, right_side, (((0,), (0,)), ((), ())), preferred_element_type=jnp.float32)

def gelu_parts(pre_values):
    normal_cdf = 0.5 * (1.0 + lax.erf(pre_values * 0.7071067811865476))
    density = jnp.exp(-0.5 * pre_values * pre_values) * 0.3989422804014327
    return (pre_values * normal_cdf, normal_cdf + pre_values * density)

def reference(patches, cotangent, preact, down_matrix, up_adapter_first, up_adapter_second, down_adapter_first, down_adapter_second):
    clip_norm = clip_scale * math.sqrt(2.0 * ADAPTER_RANK * (MODEL_FEATS + HIDDEN_UNITS))
    patch_img = patches.reshape(IMAGES, PATCHES, MODEL_FEATS)
    cot_img = cotangent.reshape(IMAGES, PATCHES, MODEL_FEATS)
    pre_img = preact.reshape(IMAGES, PATCHES, HIDDEN_UNITS)

    def one_image(totals, inputs):
        patch_row_block, cotangent_rows, pre_rows = inputs
        cotangent_rank = contract_trailing(cotangent_rows, down_adapter_second).astype(jnp.bfloat16)
        patch_by_rank = contract_trailing(patch_row_block, up_adapter_first).astype(jnp.bfloat16)
        hidden_gradient = contract_trailing(cotangent_rows, down_matrix) + jnp.dot(cotangent_rank, down_adapter_first, preferred_element_type=jnp.float32)
        activation, gelu_slope = gelu_parts(pre_rows.astype(jnp.float32))
        preact_gradient = (hidden_gradient * gelu_slope).astype(jnp.bfloat16)
        hidden_state = activation.astype(jnp.bfloat16)
        hidden_by_rank = contract_trailing(hidden_state, down_adapter_first).astype(jnp.bfloat16)
        preact_rank = contract_trailing(preact_gradient, up_adapter_second).astype(jnp.bfloat16)
        grad_a1 = contract_first(preact_rank, patch_row_block)
        grad_b1 = contract_first(patch_by_rank, preact_gradient)
        grad_a2 = contract_first(cotangent_rank, hidden_state)
        grad_b2 = contract_first(hidden_by_rank, cotangent_rows)
        grads = (grad_a1, grad_b1, grad_a2, grad_b2)
        norm_sq = jnp.float32(0.0)
        for each_grad in grads:
            norm_sq = norm_sq + jnp.sum(each_grad * each_grad)
        factor = jnp.minimum(1.0, clip_norm / jnp.sqrt(norm_sq + norm_eps))
        totals = tuple((running + factor * each_grad for running, each_grad in zip(totals, grads)))
        return (totals, preact_gradient)
    zero_sums = (jnp.zeros((ADAPTER_RANK, MODEL_FEATS), jnp.float32), jnp.zeros((ADAPTER_RANK, HIDDEN_UNITS), jnp.float32), jnp.zeros((ADAPTER_RANK, HIDDEN_UNITS), jnp.float32), jnp.zeros((ADAPTER_RANK, MODEL_FEATS), jnp.float32))
    totals, grad_rows = lax.scan(one_image, zero_sums, (patch_img, cot_img, pre_img))
    return (grad_rows.reshape(TOKENS, HIDDEN_UNITS), totals[0], totals[1], totals[2], totals[3])
```

```python
import math

import jax
import jax.numpy as jnp
from jax import lax
from jax.sharding import PartitionSpec as P

PATCHES = 256

clip_scale = 0.02
norm_eps = 1e-06

BOTH = ("dp", "tensor")
ZS, XS = 8, 4


def joint_perm(step):
    pairs = []
    for dev in range(256):
        d, t = divmod(dev, 16)
        yh, z = divmod(d, ZS)
        yl, rest = divmod(t, 8)
        x, c = divmod(rest, 2)
        yh, z, yl, x, c = step(yh, z, yl, x, c)
        pairs.append((dev, (yh * ZS + z % ZS) * 16 + yl * 8 + (x % XS) * 2 + c))
    return pairs


SWAP_CORE = joint_perm(lambda yh, z, yl, x, c: (yh, z, yl, x, 1 - c))
SWAP_YL = joint_perm(lambda yh, z, yl, x, c: (yh, z, 1 - yl, x, c))
SWAP_YH = joint_perm(lambda yh, z, yl, x, c: (1 - yh, z, yl, x, c))
RING_X = joint_perm(lambda yh, z, yl, x, c: (yh, z, yl, x + 1 - 2 * c, c))
RING_Z = joint_perm(lambda yh, z, yl, x, c: (yh, z + 1 - 2 * c, yl, x, c))


def permute(values, pairs):
    return lax.ppermute(values, BOTH, pairs)


def contract_trailing(left_side, right_side):
    return lax.dot_general(
        left_side, right_side, (((1,), (1,)), ((), ())), preferred_element_type=jnp.float32
    )


def gelu_parts(pre_values):
    normal_cdf = 0.5 * (1.0 + lax.erf(pre_values * 0.7071067811865476))
    density = jnp.exp(-0.5 * pre_values * pre_values) * 0.3989422804014327
    return (pre_values * normal_cdf, normal_cdf + pre_values * density)


def squares(values):
    return jnp.sum(values * values, axis=(1, 2))


def two_rows(value):
    high = lax.reduce_precision(value, 8, 7)
    row = lax.broadcasted_iota(jnp.int32, (1, 16, 1), 1)
    rows = jnp.where(row == 0, high[:, None, None], (value - high)[:, None, None])
    rows = jnp.where(row < 2, rows, 0.0)
    return jnp.broadcast_to(rows, (value.shape[0], 16, 256)).astype(jnp.bfloat16)


def exchange(values, axis):
    return lax.all_to_all(values, axis, split_axis=0, concat_axis=0, tiled=True)


def to_owner(rank_t):
    rank_length = rank_t.shape[0]
    by_image = rank_t.reshape(rank_length, -1, PATCHES).transpose(1, 0, 2)
    return by_image.astype(jnp.bfloat16)


def both_cores(by_image):
    n = by_image.shape[0]
    return jnp.broadcast_to(by_image[:, None], (n, 2) + by_image.shape[1:]).reshape(
        (2 * n,) + by_image.shape[1:]
    )


def on_device(
    patches,
    cotangent,
    preact,
    down_matrix,
    up_adapter_first,
    up_adapter_second,
    down_adapter_first,
    down_adapter_second,
):
    rank_length = up_adapter_second.shape[0]
    group_rows, hidden_width = preact.shape
    image_count = group_rows // PATCHES
    feat_width = patches.shape[1]
    piece_rows, piece_cols = cotangent.shape[0], down_matrix.shape[1]
    t, d = lax.axis_index("tensor"), lax.axis_index("dp")
    yl, x, c = t // 8, (t // 2) % XS, t % 2
    yh, z = d // ZS, d % ZS
    sign = 1 - 2 * c
    clip_norm = clip_scale * math.sqrt(2.0 * rank_length * (feat_width + hidden_width * 16))

    cot_all = jnp.zeros((group_rows, feat_width), jnp.bfloat16)
    down_all = jnp.zeros((hidden_width, feat_width), jnp.bfloat16)

    cot_far, down_far = permute(cotangent, SWAP_YL), permute(down_matrix, SWAP_YH)
    cot_near_sib = permute(cotangent, SWAP_CORE)
    for held, y_of in ((cotangent, yl), (cot_far, 1 - yl)):
        for j in range(XS):
            if j:
                held = permute(held, RING_X)
            sibling = cot_near_sib if held is cotangent else permute(held, SWAP_CORE)
            row = ((y_of * XS + (x - sign * j) % XS) * 2 + c) * piece_rows
            cot_all = lax.dynamic_update_slice(cot_all, held, (row, 0))
            row = ((y_of * XS + (x + sign * j) % XS) * 2 + 1 - c) * piece_rows
            cot_all = lax.dynamic_update_slice(cot_all, sibling, (row, 0))
    for held, y_of in ((down_matrix, yh), (down_far, 1 - yh)):
        for j in range(ZS):
            if j:
                held = permute(held, RING_Z)
            col = (y_of * ZS + (z - sign * j) % ZS) * piece_cols
            down_all = lax.dynamic_update_slice(down_all, held, (0, col))

    rank_rows = jnp.concatenate(
        [
            contract_trailing(down_adapter_second, cotangent),
            contract_trailing(up_adapter_first, patches),
        ],
        axis=0,
    ).astype(jnp.bfloat16)
    ranks = exchange(jnp.broadcast_to(rank_rows[None], (16,) + rank_rows.shape), "tensor")
    ranks = ranks.transpose(1, 0, 2).reshape(2 * rank_length, group_rows)
    cot_rank, patch_rank = ranks[:rank_length], ranks[rank_length:]

    def per_image(rank_part, data_part):
        return jnp.einsum(
            "rip,ipd->ird",
            rank_part.reshape(rank_length, image_count, PATCHES),
            data_part.reshape(image_count, PATCHES, hidden_width),
            preferred_element_type=jnp.float32,
        )

    activation, gelu_slope = gelu_parts(preact.astype(jnp.float32))
    hidden_state = activation.astype(jnp.bfloat16)
    hidden_parts = exchange(
        both_cores(to_owner(contract_trailing(down_adapter_first, hidden_state))), "tensor"
    )
    hidden_rank = jnp.sum(hidden_parts.astype(jnp.float32), axis=0).astype(jnp.bfloat16)
    grad_a2_each = per_image(cot_rank, hidden_state)

    def own_image(rank_part, own_rows, sibling_rows):
        near = lax.dynamic_slice_in_dim(rank_part, c * piece_rows, piece_rows, 1)
        far = lax.dynamic_slice_in_dim(rank_part, (1 - c) * piece_rows, piece_rows, 1)
        return jnp.dot(near, own_rows, preferred_element_type=jnp.float32) + jnp.dot(
            far, sibling_rows, preferred_element_type=jnp.float32
        )

    grad_b2_own = own_image(hidden_rank, cotangent, cot_near_sib)
    patches_sib = permute(patches, SWAP_CORE)

    hidden_gradient = contract_trailing(cot_all, down_all) + lax.dot_general(
        cot_rank, down_adapter_first, (((0,), (0,)), ((), ())), preferred_element_type=jnp.float32
    )
    preact_gradient = (hidden_gradient * gelu_slope).astype(jnp.bfloat16)
    grad_b1_each = per_image(patch_rank, preact_gradient)
    part_norms = squares(grad_b1_each) + squares(grad_a2_each)

    pre_parts = to_owner(contract_trailing(up_adapter_second, preact_gradient))
    pre_parts = both_cores(jnp.concatenate([pre_parts, two_rows(part_norms)], axis=1))
    summed = jnp.sum(exchange(pre_parts, "tensor").astype(jnp.float32), axis=0)
    pre_rank = summed[:rank_length].astype(jnp.bfloat16)
    grad_a1_own = own_image(pre_rank, patches, patches_sib)
    norm_sq = (
        summed[rank_length, 0]
        + summed[rank_length + 1, 0]
        + jnp.sum(grad_a1_own * grad_a1_own)
        + jnp.sum(grad_b2_own * grad_b2_own)
    )
    factor = jnp.minimum(1.0, clip_norm / jnp.sqrt(norm_sq + norm_eps))

    half = rank_length // 2

    def column_pieces(own):
        rows = lax.dynamic_slice_in_dim(own, c * half, half, 0) * factor
        return rows.reshape(half, 16, feat_width // 16).transpose(1, 0, 2).astype(jnp.bfloat16)

    factor_rows = jnp.broadcast_to(two_rows(factor[None]), (16, 16, 256))
    got = exchange(
        jnp.concatenate(
            [column_pieces(grad_a1_own), column_pieces(grad_b2_own), factor_rows], axis=1
        ),
        "tensor",
    ).astype(jnp.float32)
    got = got.reshape(image_count, 2, 2 * half + 16, 256)
    factors = got[:, 0, 2 * half, 0] + got[:, 0, 2 * half + 1, 0]
    totals = jnp.sum(got, axis=0)
    grad_a1 = totals[:, :half].reshape(rank_length, 256)
    grad_b2 = totals[:, half : 2 * half].reshape(rank_length, 256)

    def weighted_sum(each_grad):
        return jnp.sum(factors[:, None, None] * each_grad, axis=0)

    grads = jnp.concatenate(
        [grad_a1, grad_b2, weighted_sum(grad_b1_each), weighted_sum(grad_a2_each)], axis=1
    )
    pieces = grads.reshape(rank_length, 16, -1).transpose(1, 0, 2).astype(jnp.bfloat16)
    summed_piece = jnp.sum(exchange(pieces, "dp").astype(jnp.float32), axis=0)
    grads = exchange(jnp.broadcast_to(summed_piece[None], (16,) + summed_piece.shape), "dp")
    grads = grads.transpose(1, 0, 2).reshape(rank_length, -1)
    cuts = [256, 512, 512 + hidden_width]
    grad_a1, grad_b2, grad_b1, grad_a2 = jnp.split(grads, cuts, axis=1)
    return (preact_gradient, grad_a1, grad_b1, grad_a2, grad_b2)


def solution(mesh):
    placed = (
        P(("dp", "tensor"), None),
        P(("dp", "tensor"), None),
        P("dp", "tensor"),
        P("tensor", "dp"),
        P(),
        P(None, "tensor"),
        P(None, "tensor"),
        P(),
    )
    return jax.shard_map(
        on_device,
        mesh=mesh,
        in_specs=placed,
        out_specs=(
            P("dp", "tensor"),
            P(None, "tensor"),
            P(None, "tensor"),
            P(None, "tensor"),
            P(None, "tensor"),
        ),
        check_vma=False,
    )
```

```python
import functools
import math

import jax
import jax.numpy as jnp
from jax import lax
from jax.experimental import pallas as pl
from jax.experimental.pallas import tpu as pltpu
from jax.sharding import PartitionSpec as P

PATCHES = 256

clip_scale = 0.02
norm_eps = 1e-06

BOTH = ("dp", "tensor")
ZS, XS = 8, 4


def joint_perm(step):
    pairs = []
    for dev in range(256):
        d, t = divmod(dev, 16)
        yh, z = divmod(d, ZS)
        yl, rest = divmod(t, 8)
        x, c = divmod(rest, 2)
        yh, z, yl, x, c = step(yh, z, yl, x, c)
        pairs.append((dev, (yh * ZS + z % ZS) * 16 + yl * 8 + (x % XS) * 2 + c))
    return pairs


SWAP_CORE = joint_perm(lambda yh, z, yl, x, c: (yh, z, yl, x, 1 - c))
SWAP_YL = joint_perm(lambda yh, z, yl, x, c: (yh, z, 1 - yl, x, c))
SWAP_YH = joint_perm(lambda yh, z, yl, x, c: (1 - yh, z, yl, x, c))
RING_X = joint_perm(lambda yh, z, yl, x, c: (yh, z, yl, x + 1 - 2 * c, c))
RING_Z = joint_perm(lambda yh, z, yl, x, c: (yh, z + 1 - 2 * c, yl, x, c))


def permute(values, pairs):
    return lax.ppermute(values, BOTH, pairs)


def contract_trailing(left_side, right_side):
    return lax.dot_general(
        left_side, right_side, (((1,), (1,)), ((), ())), preferred_element_type=jnp.float32
    )


def gelu_parts(pre_values):
    normal_cdf = 0.5 * (1.0 + lax.erf(pre_values * 0.7071067811865476))
    density = jnp.exp(-0.5 * pre_values * pre_values) * 0.3989422804014327
    return (pre_values * normal_cdf, normal_cdf + pre_values * density)


def squares(values):
    return jnp.sum(values * values, axis=(1, 2))


def exchange(values, axis):
    return lax.all_to_all(values, axis, split_axis=0, concat_axis=0, tiled=True)


HALF_ROWS = 128


def nt(left_side, right_side):
    return contract_trailing(left_side, right_side)


def product_kernel(n, first, *refs):
    rows, cols = refs[:2]
    pieces, downs = refs[2 : 2 + n], refs[2 + n : 18 + n]
    slope, ranks, first_adapter, second_adapter = refs[18 + n : 22 + n]
    refs = refs[22 + n :]
    if not first:
        _, rank_before, b1_before = refs[:3]
        refs = refs[3:]
    grad, rank_out, b1_out, cot_v, down_v, slope_v, grad_v, cot_sem, down_sem, slope_sem, grad_sem = refs
    width = down_v.shape[0]
    block = down_v.shape[1] // 16

    def down_copy(k):
        at = pl.ds(pl.multiple_of(cols[k] * block, block), block)
        return pltpu.make_async_copy(downs[k], down_v.at[:, at], down_sem.at[k])

    def cot_copy(p):
        at = pl.ds(p * HALF_ROWS, HALF_ROWS)
        return pltpu.make_async_copy(pieces[p], cot_v.at[at], cot_sem.at[p])

    def place(p):
        return pl.ds(pl.multiple_of(rows[p] * HALF_ROWS, HALF_ROWS), HALF_ROWS)

    def held(p):
        return pl.ds(pl.multiple_of(p * HALF_ROWS, HALF_ROWS), HALF_ROWS)

    def slope_copy(p):
        return pltpu.make_async_copy(slope.at[place(p)], slope_v.at[held(p)], slope_sem.at[p])

    def grad_copy(p):
        return pltpu.make_async_copy(grad_v.at[held(p)], grad.at[place(p)], grad_sem.at[p])

    for k in range(16):
        down_copy(k).start()
    for p in range(n):
        cot_copy(p).start()
        slope_copy(p).start()
    if first:
        rank_out[...] = jnp.zeros_like(rank_out)
        b1_out[...] = jnp.zeros_like(b1_out)
    else:
        rank_out[...] = rank_before[...]
        b1_out[...] = b1_before[...]
    for k in range(16):
        down_copy(k).wait()

    @pl.loop(0, n // 2)
    def _(pair):
        for h in range(2):
            p = 2 * pair + h
            pltpu.make_async_copy(cot_v.at[held(p)], cot_v.at[held(p)], cot_sem.at[p]).wait()
            slope_copy(p).wait()
        both = pl.ds(pl.multiple_of(pair * 2 * HALF_ROWS, 2 * HALF_ROWS), 2 * HALF_ROWS)
        total = nt(cot_v[both, :], down_v[...])
        for h in range(2):
            p = 2 * pair + h
            r = rows[p]
            rank = ranks[r]
            adapter = lax.dot_general(
                rank[:32],
                first_adapter[...],
                (((0,), (0,)), ((), ())),
                preferred_element_type=jnp.float32,
            )
            part = total[h * HALF_ROWS : (h + 1) * HALF_ROWS] + adapter
            out = (part * slope_v[held(p), :]).astype(jnp.bfloat16)
            grad_v[held(p), :] = out
            grad_copy(p).start()
            rank_out[r] = nt(second_adapter[...], out)
            image = r // 2
            b1_out[image] = b1_out[image] + jnp.dot(
                rank[32:], out, preferred_element_type=jnp.float32
            )

    @pl.loop(0, n)
    def _(p):
        grad_copy(p).wait()


def product(rows, cols, pieces, downs, slope, ranks, first_adapter, second_adapter, before=None):
    n = len(pieces)
    group_rows, width = slope.shape
    feats = pieces[0].shape[1]
    vmem = pl.BlockSpec(memory_space=pltpu.VMEM)
    smem = pl.BlockSpec(memory_space=pltpu.SMEM)
    hbm = pl.BlockSpec(memory_space=pl.ANY)
    operands = [rows, cols, *pieces, *downs, slope, ranks, first_adapter, second_adapter]
    specs = [smem, smem] + [hbm] * (n + 17) + [vmem] * 3
    aliases = {}
    if before is not None:
        aliases = {len(operands): 0}
        operands += list(before)
        specs += [hbm, vmem, vmem]
    return pl.pallas_call(
        functools.partial(product_kernel, n, before is None),
        out_shape=(
            jax.ShapeDtypeStruct((group_rows, width), jnp.bfloat16),
            jax.ShapeDtypeStruct((16, 32, HALF_ROWS), jnp.float32),
            jax.ShapeDtypeStruct((8, 32, width), jnp.float32),
        ),
        in_specs=specs,
        out_specs=(hbm, vmem, vmem),
        scratch_shapes=[
            pltpu.VMEM((n * HALF_ROWS, feats), jnp.bfloat16),
            pltpu.VMEM((width, feats), jnp.bfloat16),
            pltpu.VMEM((n * HALF_ROWS, width), jnp.float32),
            pltpu.VMEM((n * HALF_ROWS, width), jnp.bfloat16),
            pltpu.SemaphoreType.DMA((n,)),
            pltpu.SemaphoreType.DMA((16,)),
            pltpu.SemaphoreType.DMA((n,)),
            pltpu.SemaphoreType.DMA((n,)),
        ],
        input_output_aliases=aliases,
        compiler_params=pltpu.CompilerParams(vmem_limit_bytes=44 * 2**20),
        cost_estimate=pl.CostEstimate(
            flops=2 * n * HALF_ROWS * width * feats,
            bytes_accessed=2 * (n * HALF_ROWS + width) * feats,
            transcendentals=0,
        ),
    )(*operands)


def in_vmem(kernel, out_shape, smem_first, *operands):
    specs = [pl.BlockSpec(memory_space=pltpu.VMEM)] * len(operands)
    if smem_first:
        specs[0] = pl.BlockSpec(memory_space=pltpu.SMEM)
    return pl.pallas_call(
        kernel,
        out_shape=out_shape,
        in_specs=specs,
        out_specs=pl.BlockSpec(memory_space=pltpu.VMEM),
        compiler_params=pltpu.CompilerParams(vmem_limit_bytes=20 * 2**20),
    )(*operands)


def own_image(c, rank_0, rank_1, own_rows, sibling_rows):
    near = jnp.where(c == 0, rank_0, rank_1).astype(jnp.bfloat16)
    far = jnp.where(c == 0, rank_1, rank_0).astype(jnp.bfloat16)
    return jnp.dot(near, own_rows, preferred_element_type=jnp.float32) + jnp.dot(
        far, sibling_rows, preferred_element_type=jnp.float32
    )


def b2_kernel(core, summed, own_rows, sibling_rows, out):
    total = jnp.sum(summed[...], axis=0)
    out[...] = own_image(core[0], total[:32], total[32:64], own_rows[...], sibling_rows[...])


def clip_kernel(clip_norm, core, got, own_rows, sibling_rows, b2, out):
    c = core[0]
    total = jnp.sum(got[...], axis=0)
    a1 = own_image(c, total[:32], total[32:64], own_rows[...], sibling_rows[...])
    norm_sq = total[64:65, 0:1] + jnp.sum(a1 * a1, keepdims=True)
    norm_sq = norm_sq + jnp.sum(b2[...] * b2[...], keepdims=True)
    factor = jnp.minimum(1.0, clip_norm / jnp.sqrt(norm_sq + norm_eps))
    high = factor.astype(jnp.bfloat16).astype(jnp.float32)
    row = lax.broadcasted_iota(jnp.int32, (16, 256), 0)
    scale = jnp.where(row == 0, high, jnp.where(row == 1, factor - high, 0.0))
    scale = scale.astype(jnp.bfloat16)
    a1_half = jnp.where(c == 0, a1[:16], a1[16:]) * factor
    b2_half = jnp.where(c == 0, b2[:16], b2[16:]) * factor
    for k in range(16):
        out[k, 0:16] = a1_half[:, k * 256 : (k + 1) * 256].astype(jnp.bfloat16)
        out[k, 16:32] = b2_half[:, k * 256 : (k + 1) * 256].astype(jnp.bfloat16)
        out[k, 32:48] = scale


def weigh_kernel(got, b1, a2, out):
    for k in range(2):
        for which in range(2):
            rows = slice(16 * which, 16 * which + 16)
            halves = []
            for core in range(2):
                part = got[core, rows].astype(jnp.float32)
                for image in range(1, 8):
                    part = part + got[2 * image + core, rows].astype(jnp.float32)
                halves.append(part[:, k * 128 : (k + 1) * 128].astype(jnp.bfloat16))
            out[2 * which + k, 0:16] = halves[0]
            out[2 * which + k, 16:32] = halves[1]
    factors = []
    for image in range(8):
        rows = got[2 * image, 32:48].astype(jnp.float32)
        factors.append(rows[0:1, 0:1] + rows[1:2, 0:1])
    for which, each in enumerate((b1, a2)):
        for k in range(6):
            cols = slice(k * 128, (k + 1) * 128)
            part = factors[0] * each[0, :, cols]
            for image in range(1, 8):
                part = part + factors[image] * each[image, :, cols]
            out[4 + 6 * which + k] = part.astype(jnp.bfloat16)


def sum_kernel(got, out):
    total = got[0].astype(jnp.float32)
    for k in range(1, 16):
        total = total + got[k].astype(jnp.float32)
    for k in range(16):
        out[k] = total


def on_device(
    patches,
    cotangent,
    preact,
    down_matrix,
    up_adapter_first,
    up_adapter_second,
    down_adapter_first,
    down_adapter_second,
):
    rank_length = up_adapter_second.shape[0]
    hidden_width = preact.shape[1]
    feat_width = patches.shape[1]
    t, d = lax.axis_index("tensor"), lax.axis_index("dp")
    yl, x, c = t // 8, (t // 2) % XS, t % 2
    yh, z = d // ZS, d % ZS
    sign = 1 - 2 * c
    core = c.astype(jnp.int32)[None]
    clip_norm = clip_scale * math.sqrt(2.0 * rank_length * (feat_width + hidden_width * 16))

    cot_far, down_far = permute(cotangent, SWAP_YL), permute(down_matrix, SWAP_YH)
    pieces, places = [], []
    for held, y_of in ((cotangent, yl), (cot_far, 1 - yl)):
        for j in range(XS):
            if j:
                held = permute(held, RING_X)
            pieces += [held, permute(held, SWAP_CORE)]
            places.append((y_of * XS + (x - sign * j) % XS) * 2 + c)
            places.append((y_of * XS + (x + sign * j) % XS) * 2 + 1 - c)
    downs, cols = [], []
    for held, y_of in ((down_matrix, yh), (down_far, 1 - yh)):
        for j in range(ZS):
            if j:
                held = permute(held, RING_Z)
            downs.append(held)
            cols.append(y_of * ZS + (z - sign * j) % ZS)
    places, cols = jnp.stack(places).astype(jnp.int32), jnp.stack(cols).astype(jnp.int32)
    cotangent_sib = pieces[1]

    rank_rows = jnp.concatenate(
        [
            contract_trailing(down_adapter_second, cotangent),
            contract_trailing(up_adapter_first, patches),
        ],
        axis=0,
    ).astype(jnp.bfloat16)
    ranks = exchange(jnp.broadcast_to(rank_rows[None], (16,) + rank_rows.shape), "tensor")

    def to_owners(rank_parts, extra=()):
        by_image = rank_parts.reshape(8, 1, 64, HALF_ROWS)
        by_image = jnp.concatenate([by_image, *extra], axis=2)
        doubled = jnp.broadcast_to(by_image, (8, 2) + by_image.shape[2:])
        return exchange(doubled.reshape((16,) + by_image.shape[2:]), "tensor")

    activation, gelu_slope = gelu_parts(preact.astype(jnp.float32))
    hidden_state = activation.astype(jnp.bfloat16)
    hidden_parts = contract_trailing(down_adapter_first, hidden_state)
    hidden_parts = hidden_parts.reshape(rank_length, 16, HALF_ROWS).transpose(1, 0, 2)
    grad_b2_own = in_vmem(
        b2_kernel,
        jax.ShapeDtypeStruct((rank_length, feat_width), jnp.float32),
        True,
        core,
        to_owners(hidden_parts),
        cotangent,
        cotangent_sib,
    )
    cot_rank = ranks[:, :rank_length].reshape(8, 2, rank_length, HALF_ROWS)
    grad_a2_each = jnp.einsum(
        "ihrp,ihpd->ird",
        cot_rank,
        hidden_state.reshape(8, 2, HALF_ROWS, hidden_width),
        preferred_element_type=jnp.float32,
    )
    a2_norms = squares(grad_a2_each)
    patches_sib = permute(patches, SWAP_CORE)

    shared = (gelu_slope, ranks, down_adapter_first, up_adapter_second)
    before = product(places[:14], cols, pieces[:14], downs, *shared)
    preact_gradient, pre_parts, grad_b1_each = product(
        places[14:], cols, pieces[14:], downs, *shared, before=before
    )
    part_norms = squares(grad_b1_each) + a2_norms

    norm_rows = jnp.broadcast_to(part_norms[:, None, None, None], (8, 1, 8, HALF_ROWS))
    clipped = in_vmem(
        functools.partial(clip_kernel, clip_norm),
        jax.ShapeDtypeStruct((16, 48, 256), jnp.bfloat16),
        True,
        core,
        to_owners(pre_parts, (norm_rows,)),
        patches,
        patches_sib,
        grad_b2_own,
    )
    group_sums = in_vmem(
        weigh_kernel,
        jax.ShapeDtypeStruct((16, rank_length, 128), jnp.bfloat16),
        False,
        exchange(clipped, "tensor"),
        grad_b1_each,
        grad_a2_each,
    )
    grads = in_vmem(
        sum_kernel,
        jax.ShapeDtypeStruct((16, rank_length, 128), jnp.float32),
        False,
        exchange(group_sums, "dp"),
    )
    grads = exchange(grads, "dp").transpose(1, 0, 2).reshape(rank_length, -1)
    cuts = [256, 512, 512 + hidden_width]
    grad_a1, grad_b2, grad_b1, grad_a2 = jnp.split(grads, cuts, axis=1)
    return (preact_gradient, grad_a1, grad_b1, grad_a2, grad_b2)


def solution(mesh):
    placed = (
        P(("dp", "tensor"), None),
        P(("dp", "tensor"), None),
        P("dp", "tensor"),
        P("tensor", "dp"),
        P(),
        P(None, "tensor"),
        P(None, "tensor"),
        P(),
    )
    return jax.shard_map(
        on_device,
        mesh=mesh,
        in_specs=placed,
        out_specs=(
            P("dp", "tensor"),
            P(None, "tensor"),
            P(None, "tensor"),
            P(None, "tensor"),
            P(None, "tensor"),
        ),
        check_vma=False,
    )
```

```python
import functools
import math

import jax
import jax.numpy as jnp
from jax import lax
from jax.experimental import pallas as pl
from jax.experimental.pallas import tpu as pltpu
from jax.sharding import PartitionSpec as P

PATCHES = 256

clip_scale = 0.02
norm_eps = 1e-06

BOTH = ("dp", "tensor")
ZS, XS = 8, 4


def joint_perm(step):
    pairs = []
    for dev in range(256):
        d, t = divmod(dev, 16)
        yh, z = divmod(d, ZS)
        yl, rest = divmod(t, 8)
        x, c = divmod(rest, 2)
        yh, z, yl, x, c = step(yh, z, yl, x, c)
        pairs.append((dev, (yh * ZS + z % ZS) * 16 + yl * 8 + (x % XS) * 2 + c))
    return pairs


SWAP_CORE = joint_perm(lambda yh, z, yl, x, c: (yh, z, yl, x, 1 - c))
SWAP_YL = joint_perm(lambda yh, z, yl, x, c: (yh, z, 1 - yl, x, c))
SWAP_YH = joint_perm(lambda yh, z, yl, x, c: (1 - yh, z, yl, x, c))
RING_X = joint_perm(lambda yh, z, yl, x, c: (yh, z, yl, x + 1 - 2 * c, c))
BACK_X = joint_perm(lambda yh, z, yl, x, c: (yh, z, yl, x - 1 + 2 * c, c))
RING_Z = joint_perm(lambda yh, z, yl, x, c: (yh, z + 1 - 2 * c, yl, x, c))


def permute(values, pairs):
    return lax.ppermute(values, BOTH, pairs)


def contract_trailing(left_side, right_side):
    return lax.dot_general(
        left_side, right_side, (((1,), (1,)), ((), ())), preferred_element_type=jnp.float32
    )


def gelu_parts(pre_values):
    normal_cdf = 0.5 * (1.0 + lax.erf(pre_values * 0.7071067811865476))
    density = jnp.exp(-0.5 * pre_values * pre_values) * 0.3989422804014327
    return (pre_values * normal_cdf, normal_cdf + pre_values * density)


def squares(values):
    return jnp.sum(values * values, axis=(1, 2))


def exchange(values, axis):
    return lax.all_to_all(values, axis, split_axis=0, concat_axis=0, tiled=True)


HALF_ROWS = 128


def nt(left_side, right_side):
    return contract_trailing(left_side, right_side)


def two_rows(value, columns):
    high = value.astype(jnp.bfloat16).astype(jnp.float32)
    row = lax.broadcasted_iota(jnp.int32, (16, columns), 0)
    rows = jnp.where(row == 0, high, jnp.where(row == 1, value - high, 0.0))
    return rows.astype(jnp.bfloat16)


def tn(left_side, right_side):
    return lax.dot_general(
        left_side, right_side, (((0,), (0,)), ((), ())), preferred_element_type=jnp.float32
    )


def product_kernel(sources, first, *refs):
    n = len(sources)
    arrays = 1 + max(part[0] for image in sources for part in image)
    images, cols, core = refs[:3]
    held, downs = refs[3 : 3 + arrays], refs[3 + arrays : 19 + arrays]
    slope, hidden, first_adapter, second_adapter = refs[19 + arrays : 23 + arrays]
    refs = refs[23 + arrays :]
    if not first:
        send_before = refs[1]
        refs = refs[4:]
    grad, send, b1_out, a2_out = refs[:4]
    cot_v, down_v, slope_v, hidden_v, grad_v, each_v, even, odd = refs[4:12]
    cot_sem, down_sem, slope_sem, hidden_sem, grad_sem, each_sem = refs[12:]
    feats = down_v.shape[1]
    block = feats // 16
    slots = cot_v.shape[0]

    def down_copy(k):
        at = pl.ds(pl.multiple_of(cols[k] * block, block), block)
        return pltpu.make_async_copy(downs[k], down_v.at[:, at], down_sem.at[k])

    def place(i):
        return pl.ds(pl.multiple_of(images[i] * PATCHES, PATCHES), PATCHES)

    def copies_in(i):
        slot = i % slots
        found = []
        for h in range(2):
            array, whose = sources[i][h]
            half = core[0] if whose == 1 else 1 - core[0]
            at = pl.ds(pl.multiple_of(half * HALF_ROWS, HALF_ROWS), HALF_ROWS)
            found.append(pltpu.make_async_copy(held[array], cot_v.at[slot, at], cot_sem.at[slot, h]))
        found.append(pltpu.make_async_copy(slope.at[place(i)], slope_v.at[slot], slope_sem.at[slot]))
        found.append(pltpu.make_async_copy(hidden.at[place(i)], hidden_v.at[slot], hidden_sem.at[slot]))
        return found

    def grad_copy(i):
        return pltpu.make_async_copy(grad_v.at[lax.rem(i, 2)], grad.at[place(i)], grad_sem.at[lax.rem(i, 2)])

    def each_copy(i, which):
        slot, to = lax.rem(i, 2), (b1_out, a2_out)[which]
        return pltpu.make_async_copy(each_v.at[slot, which], to.at[images[i]], each_sem.at[slot, which])

    def outgoing(i):
        return [grad_copy(i), each_copy(i, 0), each_copy(i, 1)]

    for copy in copies_in(0):
        copy.start()
    for k in range(16):
        down_copy(k).start()
    for i in range(1, slots - 1):
        for copy in copies_in(i):
            copy.start()
    send[...] = jnp.zeros_like(send) if first else send_before[...]
    for k in range(16):
        down_copy(k).wait()

    def arrive(i):
        slot = lax.rem(i, slots)
        for k in range(slots - 1, n):

            @pl.when(i + 1 == k)
            def _():
                for copy in copies_in(k):
                    copy.start()

        for h in range(2):
            landing = cot_v.at[slot, pl.ds(h * HALF_ROWS, HALF_ROWS)]
            pltpu.make_async_copy(landing, landing, cot_sem.at[slot, h]).wait()
        pltpu.make_async_copy(slope_v.at[slot], slope_v.at[slot], slope_sem.at[slot]).wait()
        pltpu.make_async_copy(hidden_v.at[slot], hidden_v.at[slot], hidden_sem.at[slot]).wait()
        return slot

    def finish(i, total):
        slot, way = lax.rem(i, slots), lax.rem(i, 2)
        image = images[i]
        rank_rows = cot_v[slot, :, feats:]
        adapter = jnp.dot(rank_rows[:, :32], first_adapter[...], preferred_element_type=jnp.float32)
        out = ((total[...] + adapter) * slope_v[slot]).astype(jnp.bfloat16)
        grad_v[way] = out
        rank = nt(second_adapter[...], out)
        b1 = tn(rank_rows[:, 32:64], out)
        a2 = tn(rank_rows[:, :32], hidden_v[slot])
        each_v[way, 0] = b1
        each_v[way, 1] = a2
        norm = two_rows(jnp.sum(b1 * b1 + a2 * a2, keepdims=True), HALF_ROWS)
        for to in range(2):
            send[2 * image + to, 0:32] = rank[:, :HALF_ROWS].astype(jnp.bfloat16)
            send[2 * image + to, 32:64] = rank[:, HALF_ROWS:].astype(jnp.bfloat16)
            send[2 * image + to, 64:80] = norm

    def drain(i):
        @pl.when(i > 1)
        def _():
            for copy in outgoing(i - 2):
                copy.wait()

    def step(i, now, before):
        slot = arrive(i)
        drain(i - 1)
        now[...] = nt(cot_v[slot, :, :feats], down_v[...])
        finish(i - 1, before)
        for copy in outgoing(i - 1):
            copy.start()

    slot = arrive(0)
    even[...] = nt(cot_v[slot, :, :feats], down_v[...])

    @pl.loop(1, n)
    def _(i):
        @pl.when(lax.rem(i, 2) == 1)
        def _():
            step(i, odd, even)

        @pl.when(lax.rem(i, 2) == 0)
        def _():
            step(i, even, odd)

    drain(n - 1)
    finish(n - 1, odd if n % 2 == 0 else even)
    for copy in outgoing(n - 1):
        copy.start()
    for copy in outgoing(n - 2) + outgoing(n - 1):
        copy.wait()


def product(sources, images, cols, core, held, downs, slope, hidden, adapters, before=None):
    n = len(sources)
    slots = 3
    group_rows, width = slope.shape
    feats = 16 * downs[0].shape[1]
    vmem = pl.BlockSpec(memory_space=pltpu.VMEM)
    smem = pl.BlockSpec(memory_space=pltpu.SMEM)
    hbm = pl.BlockSpec(memory_space=pl.ANY)
    stay = [pltpu.with_memory_space_constraint(v, pltpu.HBM) for v in (*held, *downs, slope, hidden)]
    operands = [images, cols, core, *stay, *adapters]
    specs = [smem] * 3 + [hbm] * len(stay) + [vmem] * 2
    each = pltpu.HBM((8, 32, width), jnp.float32)
    aliases = {}
    if before is not None:
        aliases = {len(operands) + k: k for k in (0, 2, 3)}
        operands += list(before)
        specs += [hbm, vmem, hbm, hbm]
    return pl.pallas_call(
        functools.partial(product_kernel, sources, before is None),
        out_shape=(
            jax.ShapeDtypeStruct((group_rows, width), jnp.bfloat16),
            jax.ShapeDtypeStruct((16, 80, HALF_ROWS), jnp.bfloat16),
            each,
            each,
        ),
        in_specs=specs,
        out_specs=(hbm, vmem, hbm, hbm),
        scratch_shapes=[
            pltpu.VMEM((slots, PATCHES, feats + HALF_ROWS), jnp.bfloat16),
            pltpu.VMEM((width, feats), jnp.bfloat16),
            pltpu.VMEM((slots, PATCHES, width), jnp.float32),
            pltpu.VMEM((slots, PATCHES, width), jnp.bfloat16),
            pltpu.VMEM((2, PATCHES, width), jnp.bfloat16),
            pltpu.VMEM((2, 2, 32, width), jnp.float32),
            pltpu.VMEM((PATCHES, width), jnp.float32),
            pltpu.VMEM((PATCHES, width), jnp.float32),
            pltpu.SemaphoreType.DMA((slots, 2)),
            pltpu.SemaphoreType.DMA((16,)),
            pltpu.SemaphoreType.DMA((slots,)),
            pltpu.SemaphoreType.DMA((slots,)),
            pltpu.SemaphoreType.DMA((2,)),
            pltpu.SemaphoreType.DMA((2, 2)),
        ],
        input_output_aliases=aliases,
        compiler_params=pltpu.CompilerParams(vmem_limit_bytes=40 * 2**20),
        cost_estimate=pl.CostEstimate(
            flops=2 * n * PATCHES * width * feats,
            bytes_accessed=2 * (n * PATCHES + width) * feats,
            transcendentals=0,
        ),
    )(*operands)


def in_vmem(kernel, out_shape, small, large=()):
    count, wide = len(small), len(large)

    def body(*refs):
        out, landed, sems = refs[count + wide], refs[count + wide + 1 : -1], refs[-1]
        copies = [
            pltpu.make_async_copy(refs[count + k], landed[k], sems.at[k]) for k in range(wide)
        ]
        for copy in copies:
            copy.start()
        for copy in copies:
            copy.wait()
        kernel(*refs[:count], *landed, out)

    specs = [
        pl.BlockSpec(memory_space=pltpu.SMEM if v.dtype == jnp.int32 else pltpu.VMEM) for v in small
    ]
    return pl.pallas_call(
        body,
        out_shape=out_shape,
        in_specs=specs + [pl.BlockSpec(memory_space=pl.ANY)] * wide,
        out_specs=pl.BlockSpec(memory_space=pltpu.VMEM),
        scratch_shapes=[pltpu.VMEM(v.shape, v.dtype) for v in large]
        + [pltpu.SemaphoreType.DMA((max(wide, 1),))],
        compiler_params=pltpu.CompilerParams(vmem_limit_bytes=20 * 2**20),
    )(*small, *(pltpu.with_memory_space_constraint(v, pltpu.HBM) for v in large))


def own_image(c, rank_0, rank_1, own_rows, sibling_rows):
    near = jnp.where(c == 0, rank_0, rank_1).astype(jnp.bfloat16)
    far = jnp.where(c == 0, rank_1, rank_0).astype(jnp.bfloat16)
    return jnp.dot(near, own_rows, preferred_element_type=jnp.float32) + jnp.dot(
        far, sibling_rows, preferred_element_type=jnp.float32
    )


def rank_kernel(cot_adapter, patch_adapter, cotangent, patches, out):
    ranks = [nt(cotangent[...], cot_adapter[...]), nt(patches[...], patch_adapter[...])]
    ranks.append(jnp.zeros((cotangent.shape[0], 64), jnp.float32))
    feats = cotangent.shape[1]
    out[:, :feats] = cotangent[...]
    out[:, feats:] = jnp.concatenate(ranks, axis=1).astype(jnp.bfloat16)


def b2_kernel(near, far, own_rows, sibling_rows, out):
    out[...] = jnp.dot(near[...], own_rows[...], preferred_element_type=jnp.float32) + jnp.dot(
        far[...], sibling_rows[:, : out.shape[1]], preferred_element_type=jnp.float32
    )


def clip_kernel(clip_norm, core, got, b2, own_rows, sibling_rows, out):
    c = core[0]
    total = got[0].astype(jnp.float32)
    for k in range(1, 16):
        total = total + got[k].astype(jnp.float32)
    a1 = own_image(c, total[:32], total[32:64], own_rows[...], sibling_rows[...])
    norm_sq = total[64:65, 0:1] + total[65:66, 0:1] + jnp.sum(a1 * a1, keepdims=True)
    norm_sq = norm_sq + jnp.sum(b2[...] * b2[...], keepdims=True)
    factor = jnp.minimum(1.0, clip_norm / jnp.sqrt(norm_sq + norm_eps))
    scale = two_rows(factor, 256)
    a1_half = jnp.where(c == 0, a1[:16], a1[16:]) * factor
    b2_half = jnp.where(c == 0, b2[:16], b2[16:]) * factor
    for k in range(16):
        out[k, 0:16] = a1_half[:, k * 256 : (k + 1) * 256].astype(jnp.bfloat16)
        out[k, 16:32] = b2_half[:, k * 256 : (k + 1) * 256].astype(jnp.bfloat16)
        out[k, 32:48] = scale


def weigh_kernel(got, b1, a2, out):
    for k in range(2):
        for which in range(2):
            rows = slice(16 * which, 16 * which + 16)
            halves = []
            for core in range(2):
                part = got[core, rows].astype(jnp.float32)
                for image in range(1, 8):
                    part = part + got[2 * image + core, rows].astype(jnp.float32)
                halves.append(part[:, k * 128 : (k + 1) * 128].astype(jnp.bfloat16))
            out[2 * which + k, 0:16] = halves[0]
            out[2 * which + k, 16:32] = halves[1]
    factors = []
    for image in range(8):
        rows = got[2 * image, 32:48].astype(jnp.float32)
        factors.append(rows[0:1, 0:1] + rows[1:2, 0:1])
    for which, each in enumerate((b1, a2)):
        for k in range(6):
            cols = slice(k * 128, (k + 1) * 128)
            part = factors[0] * each[0, :, cols]
            for image in range(1, 8):
                part = part + factors[image] * each[image, :, cols]
            out[4 + 6 * which + k] = part.astype(jnp.bfloat16)


def sum_kernel(got, out):
    total = got[0].astype(jnp.float32)
    for k in range(1, 16):
        total = total + got[k].astype(jnp.float32)
    for k in range(16):
        out[k] = total


def on_device(
    patches,
    cotangent,
    preact,
    down_matrix,
    up_adapter_first,
    up_adapter_second,
    down_adapter_first,
    down_adapter_second,
):
    rank_length = up_adapter_second.shape[0]
    hidden_width = preact.shape[1]
    feat_width = patches.shape[1]
    t, d = lax.axis_index("tensor"), lax.axis_index("dp")
    yl, x, c = t // 8, (t // 2) % XS, t % 2
    yh, z = d // ZS, d % ZS
    sign = 1 - 2 * c
    core = c.astype(jnp.int32)[None]
    clip_norm = clip_scale * math.sqrt(2.0 * rank_length * (feat_width + hidden_width * 16))

    kept, last = {}, None

    def received(name, value):
        nonlocal last
        if last is not None:
            value, kept[last] = lax.optimization_barrier((value, kept[last]))
        kept[name], last = value, name
        return value

    def after(value):
        value, kept[last] = lax.optimization_barrier((value, kept[last]))
        return value

    def swapped(value):
        return permute(value, SWAP_CORE)

    flying = {"E0": permute(down_matrix, SWAP_YH), "D1": permute(down_matrix, RING_Z)}
    def swap(name):
        flying["s" + name] = swapped(after(kept[name]))

    own_rows = in_vmem(
        rank_kernel,
        jax.ShapeDtypeStruct((cotangent.shape[0], feat_width + HALF_ROWS), jnp.bfloat16),
        (),
        (down_adapter_second, up_adapter_first, cotangent, patches),
    )
    kept["A0"], last = own_rows, "A0"
    flying["A1"], flying["A3"] = permute(own_rows, RING_X), permute(own_rows, BACK_X)
    onward = {
        "A1": [("A2", RING_X)],
        "A2": [("B2", SWAP_YL)],
        "B0": [("B1", RING_X), ("B3", BACK_X)],
    }

    def land(name):
        held = received(name, flying.pop(name))
        series, number = name[0], name[1:]
        if series in "DE" and int(number) < ZS - 1:
            flying[f"{series}{int(number) + 1}"] = permute(held, RING_Z)
        for to, pairs in onward.get(name, ()):
            flying[to] = permute(held, pairs)

    land("D1")
    land("E0")
    flying["B0"] = permute(after(own_rows), SWAP_YL)
    activation, gelu_slope = gelu_parts(after(preact).astype(jnp.float32))
    hidden_state = activation.astype(jnp.bfloat16)
    received("hidden", hidden_state)
    land("D2")
    land("E1")
    hidden_parts = contract_trailing(down_adapter_first, kept["hidden"])
    hidden_parts = hidden_parts.reshape(rank_length, 16, HALF_ROWS).transpose(1, 0, 2)
    high = lax.reduce_precision(hidden_parts, 8, 7)
    early = jnp.concatenate(
        [high.astype(jnp.bfloat16), (hidden_parts - high).astype(jnp.bfloat16)], axis=1
    )
    received("early", early)
    for name in ("D3", "E2", "A1", "A3", "D4", "E3", "B0", "D5", "A2", "E4", "D6", "E5", "D7"):
        land(name)
    for name in ("B1", "B3", "B2", "E6"):
        land(name)
    for j in range(XS):
        swap(f"A{j}")
    land("E7")
    for j in range(XS):
        swap(f"B{j}")
    got = exchange(kept["early"], "tensor")

    downs = [down_matrix] + [kept[f"D{j}"] for j in range(1, ZS)] + [kept[f"E{j}"] for j in range(ZS)]
    cols = [y * ZS + (z - sign * j) % ZS for y in (yh, 1 - yh) for j in range(ZS)]
    cols = jnp.stack(cols).astype(jnp.int32)

    def sibling(name):
        return kept[name] if name in kept else flying[name]

    held, sources, images = [], [], []
    for series, y_of in (("A", yl), ("B", 1 - yl)):
        for j in range(XS):
            sources.append(((len(held), 1), (len(held) + 1, -1)))
            held += [kept[f"{series}{j}"], sibling(f"s{series}{-j % XS}")]
            images.append(y_of * XS + (x - sign * j) % XS)
    patches_sib = swapped(after(patches))
    preact_gradient, to_owners, grad_b1_each, grad_a2_each = product(
        sources,
        jnp.stack(images).astype(jnp.int32),
        cols,
        core,
        held,
        downs,
        gelu_slope,
        kept["hidden"],
        (down_adapter_first, up_adapter_second),
    )
    got, to_owners = lax.optimization_barrier((got, to_owners))
    summed = jnp.sum(got.astype(jnp.float32), axis=0)
    hidden_rank = (summed[:rank_length] + summed[rank_length:]).astype(jnp.bfloat16)
    grad_b2_own = in_vmem(
        b2_kernel,
        jax.ShapeDtypeStruct((rank_length, feat_width), jnp.float32),
        (hidden_rank, swapped(hidden_rank)),
        (cotangent, flying["sA0"]),
    )

    clipped = in_vmem(
        functools.partial(clip_kernel, clip_norm),
        jax.ShapeDtypeStruct((16, 48, 256), jnp.bfloat16),
        (core, exchange(to_owners, "tensor"), grad_b2_own),
        (patches, patches_sib),
    )
    group_sums = in_vmem(
        weigh_kernel,
        jax.ShapeDtypeStruct((16, rank_length, 128), jnp.bfloat16),
        (exchange(clipped, "tensor"),),
        (grad_b1_each, grad_a2_each),
    )
    grads = in_vmem(
        sum_kernel,
        jax.ShapeDtypeStruct((16, rank_length, 128), jnp.float32),
        (exchange(group_sums, "dp"),),
    )
    grads = exchange(grads, "dp").transpose(1, 0, 2).reshape(rank_length, -1)
    cuts = [256, 512, 512 + hidden_width]
    grad_a1, grad_b2, grad_b1, grad_a2 = jnp.split(grads, cuts, axis=1)
    return (preact_gradient, grad_a1, grad_b1, grad_a2, grad_b2)


def solution(mesh):
    placed = (
        P(("dp", "tensor"), None),
        P(("dp", "tensor"), None),
        P("dp", "tensor"),
        P("tensor", "dp"),
        P(),
        P(None, "tensor"),
        P(None, "tensor"),
        P(),
    )
    return jax.shard_map(
        on_device,
        mesh=mesh,
        in_specs=placed,
        out_specs=(
            P("dp", "tensor"),
            P(None, "tensor"),
            P(None, "tensor"),
            P(None, "tensor"),
            P(None, "tensor"),
        ),
        check_vma=False,
    )
```

```python
import functools
import math

import jax
import jax.numpy as jnp
from jax import lax
from jax.experimental import pallas as pl
from jax.experimental.pallas import tpu as pltpu
from jax.sharding import PartitionSpec as P

PATCHES = 256

clip_scale = 0.02
norm_eps = 1e-06

BOTH = ("dp", "tensor")
ZS, XS = 8, 4


def joint_perm(step):
    pairs = []
    for dev in range(256):
        d, t = divmod(dev, 16)
        yh, z = divmod(d, ZS)
        yl, rest = divmod(t, 8)
        x, c = divmod(rest, 2)
        yh, z, yl, x, c = step(yh, z, yl, x, c)
        pairs.append((dev, (yh * ZS + z % ZS) * 16 + yl * 8 + (x % XS) * 2 + c))
    return pairs


SWAP_CORE = joint_perm(lambda yh, z, yl, x, c: (yh, z, yl, x, 1 - c))
SWAP_YL = joint_perm(lambda yh, z, yl, x, c: (yh, z, 1 - yl, x, c))
SWAP_YH = joint_perm(lambda yh, z, yl, x, c: (1 - yh, z, yl, x, c))
RING_X = joint_perm(lambda yh, z, yl, x, c: (yh, z, yl, x + 1 - 2 * c, c))
BACK_X = joint_perm(lambda yh, z, yl, x, c: (yh, z, yl, x - 1 + 2 * c, c))
BACK_Z = joint_perm(lambda yh, z, yl, x, c: (yh, z - 1 + 2 * c, yl, x, c))
RING_Z = joint_perm(lambda yh, z, yl, x, c: (yh, z + 1 - 2 * c, yl, x, c))


def permute(values, pairs):
    return lax.ppermute(values, BOTH, pairs)


def contract_trailing(left_side, right_side):
    return lax.dot_general(
        left_side, right_side, (((1,), (1,)), ((), ())), preferred_element_type=jnp.float32
    )


def gelu_parts(pre_values):
    normal_cdf = 0.5 * (1.0 + lax.erf(pre_values * 0.7071067811865476))
    density = jnp.exp(-0.5 * pre_values * pre_values) * 0.3989422804014327
    return (pre_values * normal_cdf, normal_cdf + pre_values * density)


def squares(values):
    return jnp.sum(values * values, axis=(1, 2))


def exchange(values, axis):
    return lax.all_to_all(values, axis, split_axis=0, concat_axis=0, tiled=True)


HALF_ROWS = 128


def nt(left_side, right_side):
    return contract_trailing(left_side, right_side)


def two_rows(value, columns):
    high = value.astype(jnp.bfloat16).astype(jnp.float32)
    row = lax.broadcasted_iota(jnp.int32, (16, columns), 0)
    rows = jnp.where(row == 0, high, jnp.where(row == 1, value - high, 0.0))
    return rows.astype(jnp.bfloat16)


def tn(left_side, right_side):
    return lax.dot_general(
        left_side, right_side, (((0,), (0,)), ((), ())), preferred_element_type=jnp.float32
    )


def product_kernel(sources, first, *refs):
    n = len(sources)
    arrays = 1 + max(part[0] for image in sources for part in image)
    images, cols, core = refs[:3]
    held, downs = refs[3 : 3 + arrays], refs[3 + arrays : 19 + arrays]
    slope, hidden, first_adapter, second_adapter = refs[19 + arrays : 23 + arrays]
    refs = refs[23 + arrays :]
    if not first:
        send_before = refs[1]
        refs = refs[4:]
    grad, send, b1_out, a2_out = refs[:4]
    cot_v, down_v, slope_v, hidden_v, grad_v, each_v, even, odd = refs[4:12]
    cot_sem, down_sem, slope_sem, hidden_sem, grad_sem, each_sem = refs[12:]
    feats = down_v.shape[1]
    block = feats // 16
    slots = cot_v.shape[0]

    def down_copy(k):
        at = pl.ds(pl.multiple_of(cols[k] * block, block), block)
        return pltpu.make_async_copy(downs[k], down_v.at[:, at], down_sem.at[k])

    def place(i):
        return pl.ds(pl.multiple_of(images[i] * PATCHES, PATCHES), PATCHES)

    def copies_in(i):
        slot = i % slots
        found = []
        for h in range(2):
            array, whose = sources[i][h]
            half = core[0] if whose == 1 else 1 - core[0]
            at = pl.ds(pl.multiple_of(half * HALF_ROWS, HALF_ROWS), HALF_ROWS)
            found.append(pltpu.make_async_copy(held[array], cot_v.at[slot, at], cot_sem.at[slot, h]))
        found.append(pltpu.make_async_copy(slope.at[place(i)], slope_v.at[slot], slope_sem.at[slot]))
        found.append(pltpu.make_async_copy(hidden.at[place(i)], hidden_v.at[slot], hidden_sem.at[slot]))
        return found

    def grad_copy(i):
        return pltpu.make_async_copy(grad_v.at[lax.rem(i, 2)], grad.at[place(i)], grad_sem.at[lax.rem(i, 2)])

    def each_copy(i, which):
        slot, to = lax.rem(i, 2), (b1_out, a2_out)[which]
        return pltpu.make_async_copy(each_v.at[slot, which], to.at[images[i]], each_sem.at[slot, which])

    def outgoing(i):
        return [grad_copy(i), each_copy(i, 0), each_copy(i, 1)]

    for copy in copies_in(0):
        copy.start()
    for k in range(16):
        down_copy(k).start()
    for i in range(1, slots - 1):
        for copy in copies_in(i):
            copy.start()
    send[...] = jnp.zeros_like(send) if first else send_before[...]
    for k in range(16):
        down_copy(k).wait()

    def arrive(i):
        slot = lax.rem(i, slots)
        for k in range(slots - 1, n):

            @pl.when(i + 1 == k)
            def _():
                for copy in copies_in(k):
                    copy.start()

        for h in range(2):
            landing = cot_v.at[slot, pl.ds(h * HALF_ROWS, HALF_ROWS)]
            pltpu.make_async_copy(landing, landing, cot_sem.at[slot, h]).wait()
        pltpu.make_async_copy(slope_v.at[slot], slope_v.at[slot], slope_sem.at[slot]).wait()
        pltpu.make_async_copy(hidden_v.at[slot], hidden_v.at[slot], hidden_sem.at[slot]).wait()
        return slot

    def finish(i, total):
        slot, way = lax.rem(i, slots), lax.rem(i, 2)
        image = images[i]
        rank_rows = cot_v[slot, :, feats:]
        adapter = jnp.dot(rank_rows[:, :32], first_adapter[...], preferred_element_type=jnp.float32)
        out = ((total[...] + adapter) * slope_v[slot]).astype(jnp.bfloat16)
        grad_v[way] = out
        rank = nt(second_adapter[...], out)
        b1 = tn(rank_rows[:, 32:64], out)
        a2 = tn(rank_rows[:, :32], hidden_v[slot])
        each_v[way, 0] = b1
        each_v[way, 1] = a2
        norm = two_rows(jnp.sum(b1 * b1 + a2 * a2, keepdims=True), HALF_ROWS)
        for to in range(2):
            send[2 * image + to, 0:32] = rank[:, :HALF_ROWS].astype(jnp.bfloat16)
            send[2 * image + to, 32:64] = rank[:, HALF_ROWS:].astype(jnp.bfloat16)
            send[2 * image + to, 64:80] = norm

    def drain(i):
        @pl.when(i > 1)
        def _():
            for copy in outgoing(i - 2):
                copy.wait()

    def step(i, now, before):
        slot = arrive(i)
        drain(i - 1)
        now[...] = nt(cot_v[slot, :, :feats], down_v[...])
        finish(i - 1, before)
        for copy in outgoing(i - 1):
            copy.start()

    slot = arrive(0)
    even[...] = nt(cot_v[slot, :, :feats], down_v[...])

    @pl.loop(1, n)
    def _(i):
        @pl.when(lax.rem(i, 2) == 1)
        def _():
            step(i, odd, even)

        @pl.when(lax.rem(i, 2) == 0)
        def _():
            step(i, even, odd)

    drain(n - 1)
    finish(n - 1, odd if n % 2 == 0 else even)
    for copy in outgoing(n - 1):
        copy.start()
    for copy in outgoing(n - 2) + outgoing(n - 1):
        copy.wait()


def product(sources, images, cols, core, held, downs, slope, hidden, adapters, before=None):
    n = len(sources)
    slots = 3
    group_rows, width = slope.shape
    feats = 16 * downs[0].shape[1]
    vmem = pl.BlockSpec(memory_space=pltpu.VMEM)
    smem = pl.BlockSpec(memory_space=pltpu.SMEM)
    hbm = pl.BlockSpec(memory_space=pl.ANY)
    stay = [pltpu.with_memory_space_constraint(v, pltpu.HBM) for v in (*held, *downs, slope, hidden)]
    operands = [images, cols, core, *stay, *adapters]
    specs = [smem] * 3 + [hbm] * len(stay) + [vmem] * 2
    each = pltpu.HBM((8, 32, width), jnp.float32)
    aliases = {}
    if before is not None:
        aliases = {len(operands) + k: k for k in (0, 2, 3)}
        operands += list(before)
        specs += [hbm, vmem, hbm, hbm]
    return pl.pallas_call(
        functools.partial(product_kernel, sources, before is None),
        out_shape=(
            jax.ShapeDtypeStruct((group_rows, width), jnp.bfloat16),
            jax.ShapeDtypeStruct((16, 80, HALF_ROWS), jnp.bfloat16),
            each,
            each,
        ),
        in_specs=specs,
        out_specs=(hbm, vmem, hbm, hbm),
        scratch_shapes=[
            pltpu.VMEM((slots, PATCHES, feats + HALF_ROWS), jnp.bfloat16),
            pltpu.VMEM((width, feats), jnp.bfloat16),
            pltpu.VMEM((slots, PATCHES, width), jnp.float32),
            pltpu.VMEM((slots, PATCHES, width), jnp.bfloat16),
            pltpu.VMEM((2, PATCHES, width), jnp.bfloat16),
            pltpu.VMEM((2, 2, 32, width), jnp.float32),
            pltpu.VMEM((PATCHES, width), jnp.float32),
            pltpu.VMEM((PATCHES, width), jnp.float32),
            pltpu.SemaphoreType.DMA((slots, 2)),
            pltpu.SemaphoreType.DMA((16,)),
            pltpu.SemaphoreType.DMA((slots,)),
            pltpu.SemaphoreType.DMA((slots,)),
            pltpu.SemaphoreType.DMA((2,)),
            pltpu.SemaphoreType.DMA((2, 2)),
        ],
        input_output_aliases=aliases,
        compiler_params=pltpu.CompilerParams(vmem_limit_bytes=40 * 2**20),
        cost_estimate=pl.CostEstimate(
            flops=2 * n * PATCHES * width * feats,
            bytes_accessed=2 * (n * PATCHES + width) * feats,
            transcendentals=0,
        ),
    )(*operands)


def in_vmem(kernel, out_shape, small, large=()):
    count, wide = len(small), len(large)

    def body(*refs):
        out, landed, sems = refs[count + wide], refs[count + wide + 1 : -1], refs[-1]
        copies = [
            pltpu.make_async_copy(refs[count + k], landed[k], sems.at[k]) for k in range(wide)
        ]
        for copy in copies:
            copy.start()
        for copy in copies:
            copy.wait()
        kernel(*refs[:count], *landed, out)

    specs = [
        pl.BlockSpec(memory_space=pltpu.SMEM if v.dtype == jnp.int32 else pltpu.VMEM) for v in small
    ]
    return pl.pallas_call(
        body,
        out_shape=out_shape,
        in_specs=specs + [pl.BlockSpec(memory_space=pl.ANY)] * wide,
        out_specs=pl.BlockSpec(memory_space=pltpu.VMEM),
        scratch_shapes=[pltpu.VMEM(v.shape, v.dtype) for v in large]
        + [pltpu.SemaphoreType.DMA((max(wide, 1),))],
        compiler_params=pltpu.CompilerParams(vmem_limit_bytes=20 * 2**20),
    )(*small, *(pltpu.with_memory_space_constraint(v, pltpu.HBM) for v in large))


def own_image(c, rank_0, rank_1, own_rows, sibling_rows):
    near = jnp.where(c == 0, rank_0, rank_1).astype(jnp.bfloat16)
    far = jnp.where(c == 0, rank_1, rank_0).astype(jnp.bfloat16)
    return jnp.dot(near, own_rows, preferred_element_type=jnp.float32) + jnp.dot(
        far, sibling_rows, preferred_element_type=jnp.float32
    )


def rank_kernel(cot_adapter, patch_adapter, cotangent, patches, out):
    ranks = [nt(cotangent[...], cot_adapter[...]), nt(patches[...], patch_adapter[...])]
    ranks.append(jnp.zeros((cotangent.shape[0], 64), jnp.float32))
    feats = cotangent.shape[1]
    out[:, :feats] = cotangent[...]
    out[:, feats:] = jnp.concatenate(ranks, axis=1).astype(jnp.bfloat16)


def b2_kernel(near, far, own_rows, sibling_rows, out):
    out[...] = jnp.dot(near[...], own_rows[...], preferred_element_type=jnp.float32) + jnp.dot(
        far[...], sibling_rows[:, : out.shape[1]], preferred_element_type=jnp.float32
    )


def clip_kernel(clip_norm, core, got, b2, own_rows, sibling_rows, out):
    c = core[0]
    total = got[0].astype(jnp.float32)
    for k in range(1, 16):
        total = total + got[k].astype(jnp.float32)
    a1 = own_image(c, total[:32], total[32:64], own_rows[...], sibling_rows[...])
    norm_sq = total[64:65, 0:1] + total[65:66, 0:1] + jnp.sum(a1 * a1, keepdims=True)
    norm_sq = norm_sq + jnp.sum(b2[...] * b2[...], keepdims=True)
    factor = jnp.minimum(1.0, clip_norm / jnp.sqrt(norm_sq + norm_eps))
    scale = two_rows(factor, 256)
    a1_half = jnp.where(c == 0, a1[:16], a1[16:]) * factor
    b2_half = jnp.where(c == 0, b2[:16], b2[16:]) * factor
    for k in range(16):
        out[k, 0:16] = a1_half[:, k * 256 : (k + 1) * 256].astype(jnp.bfloat16)
        out[k, 16:32] = b2_half[:, k * 256 : (k + 1) * 256].astype(jnp.bfloat16)
        out[k, 32:48] = scale


def weigh_kernel(got, b1, a2, out):
    for k in range(2):
        for which in range(2):
            rows = slice(16 * which, 16 * which + 16)
            halves = []
            for core in range(2):
                part = got[core, rows].astype(jnp.float32)
                for image in range(1, 8):
                    part = part + got[2 * image + core, rows].astype(jnp.float32)
                halves.append(part[:, k * 128 : (k + 1) * 128].astype(jnp.bfloat16))
            out[2 * which + k, 0:16] = halves[0]
            out[2 * which + k, 16:32] = halves[1]
    factors = []
    for image in range(8):
        rows = got[2 * image, 32:48].astype(jnp.float32)
        factors.append(rows[0:1, 0:1] + rows[1:2, 0:1])
    for which, each in enumerate((b1, a2)):
        for k in range(6):
            cols = slice(k * 128, (k + 1) * 128)
            part = factors[0] * each[0, :, cols]
            for image in range(1, 8):
                part = part + factors[image] * each[image, :, cols]
            out[4 + 6 * which + k] = part.astype(jnp.bfloat16)


def sum_kernel(got, out):
    total = got[0].astype(jnp.float32)
    for k in range(1, 16):
        total = total + got[k].astype(jnp.float32)
    for k in range(16):
        out[k] = total


def on_device(
    patches,
    cotangent,
    preact,
    down_matrix,
    up_adapter_first,
    up_adapter_second,
    down_adapter_first,
    down_adapter_second,
):
    rank_length = up_adapter_second.shape[0]
    hidden_width = preact.shape[1]
    feat_width = patches.shape[1]
    t, d = lax.axis_index("tensor"), lax.axis_index("dp")
    yl, x, c = t // 8, (t // 2) % XS, t % 2
    yh, z = d // ZS, d % ZS
    sign = 1 - 2 * c
    core = c.astype(jnp.int32)[None]
    clip_norm = clip_scale * math.sqrt(2.0 * rank_length * (feat_width + hidden_width * 16))

    kept, last = {}, None

    def received(name, value):
        nonlocal last
        if last is not None:
            value, kept[last] = lax.optimization_barrier((value, kept[last]))
        kept[name], last = value, name
        return value

    def after(value):
        value, kept[last] = lax.optimization_barrier((value, kept[last]))
        return value

    def swapped(value):
        return permute(value, SWAP_CORE)

    flying = {"E0": permute(down_matrix, SWAP_YH), "D1": permute(down_matrix, RING_Z)}
    def swap(name):
        flying["s" + name] = swapped(after(kept[name]))

    own_rows = in_vmem(
        rank_kernel,
        jax.ShapeDtypeStruct((cotangent.shape[0], feat_width + HALF_ROWS), jnp.bfloat16),
        (),
        (down_adapter_second, up_adapter_first, cotangent, patches),
    )
    kept["A0"], last = own_rows, "A0"
    flying["A1"], flying["A3"] = permute(own_rows, RING_X), permute(own_rows, BACK_X)
    onward = {
        "A1": [("A2", RING_X)],
        "A2": [("B2", SWAP_YL)],
        "B0": [("B1", RING_X), ("B3", BACK_X)],
    }

    def land(name):
        held = received(name, flying.pop(name))
        series, number = name[0], name[1:]
        if series in "DE" and int(number) < ZS - (1 if series == "D" else 2):
            flying[f"{series}{int(number) + 1}"] = permute(held, RING_Z)
        for to, pairs in onward.get(name, ()):
            flying[to] = permute(held, pairs)

    land("D1")
    land("E0")
    flying["B0"] = permute(after(own_rows), SWAP_YL)
    activation, gelu_slope = gelu_parts(after(preact).astype(jnp.float32))
    hidden_state = activation.astype(jnp.bfloat16)
    received("hidden", hidden_state)
    land("D2")
    land("E1")
    hidden_parts = contract_trailing(down_adapter_first, kept["hidden"])
    hidden_parts = hidden_parts.reshape(rank_length, 16, HALF_ROWS).transpose(1, 0, 2)
    high = lax.reduce_precision(hidden_parts, 8, 7)
    early = jnp.concatenate(
        [high.astype(jnp.bfloat16), (hidden_parts - high).astype(jnp.bfloat16)], axis=1
    )
    received("early", early)
    for name in ("D3", "E2", "A1", "A3", "D4", "E3", "B0", "A2", "D5", "E4", "D6", "E5", "D7"):
        land(name)
    flying["E7"] = permute(after(kept["E0"]), BACK_Z)
    for name in ("B1", "B3", "B2", "E6"):
        land(name)
    for j in range(XS):
        swap(f"A{j}")
    land("E7")
    for j in range(XS):
        swap(f"B{j}")
    got = exchange(kept["early"], "tensor")

    downs = [down_matrix] + [kept[f"D{j}"] for j in range(1, ZS)] + [kept[f"E{j}"] for j in range(ZS)]
    cols = [y * ZS + (z - sign * j) % ZS for y in (yh, 1 - yh) for j in range(ZS)]
    cols = jnp.stack(cols).astype(jnp.int32)

    def sibling(name):
        return kept[name] if name in kept else flying[name]

    held, sources, images = [], [], []
    for series, y_of in (("A", yl), ("B", 1 - yl)):
        for j in range(XS):
            sources.append(((len(held), 1), (len(held) + 1, -1)))
            held += [kept[f"{series}{j}"], sibling(f"s{series}{-j % XS}")]
            images.append(y_of * XS + (x - sign * j) % XS)
    patches_sib = swapped(after(patches))
    preact_gradient, to_owners, grad_b1_each, grad_a2_each = product(
        sources,
        jnp.stack(images).astype(jnp.int32),
        cols,
        core,
        held,
        downs,
        gelu_slope,
        kept["hidden"],
        (down_adapter_first, up_adapter_second),
    )
    got, to_owners = lax.optimization_barrier((got, to_owners))
    summed = jnp.sum(got.astype(jnp.float32), axis=0)
    hidden_rank = (summed[:rank_length] + summed[rank_length:]).astype(jnp.bfloat16)
    grad_b2_own = in_vmem(
        b2_kernel,
        jax.ShapeDtypeStruct((rank_length, feat_width), jnp.float32),
        (hidden_rank, swapped(hidden_rank)),
        (cotangent, flying["sA0"]),
    )

    clipped = in_vmem(
        functools.partial(clip_kernel, clip_norm),
        jax.ShapeDtypeStruct((16, 48, 256), jnp.bfloat16),
        (core, exchange(to_owners, "tensor"), grad_b2_own),
        (patches, patches_sib),
    )
    group_sums = in_vmem(
        weigh_kernel,
        jax.ShapeDtypeStruct((16, rank_length, 128), jnp.bfloat16),
        (exchange(clipped, "tensor"),),
        (grad_b1_each, grad_a2_each),
    )
    grads = in_vmem(
        sum_kernel,
        jax.ShapeDtypeStruct((16, rank_length, 128), jnp.float32),
        (exchange(group_sums, "dp"),),
    )
    grads = exchange(grads, "dp").transpose(1, 0, 2).reshape(rank_length, -1)
    cuts = [256, 512, 512 + hidden_width]
    grad_a1, grad_b2, grad_b1, grad_a2 = jnp.split(grads, cuts, axis=1)
    return (preact_gradient, grad_a1, grad_b1, grad_a2, grad_b2)


def solution(mesh):
    placed = (
        P(("dp", "tensor"), None),
        P(("dp", "tensor"), None),
        P("dp", "tensor"),
        P("tensor", "dp"),
        P(),
        P(None, "tensor"),
        P(None, "tensor"),
        P(),
    )
    return jax.shard_map(
        on_device,
        mesh=mesh,
        in_specs=placed,
        out_specs=(
            P("dp", "tensor"),
            P(None, "tensor"),
            P(None, "tensor"),
            P(None, "tensor"),
            P(None, "tensor"),
        ),
        check_vma=False,
    )
```

```python
import functools
import math

import jax
import jax.numpy as jnp
from jax import lax
from jax.experimental import pallas as pl
from jax.experimental.pallas import tpu as pltpu
from jax.sharding import PartitionSpec as P

PATCHES = 256

clip_scale = 0.02
norm_eps = 1e-06

BOTH = ("dp", "tensor")
ZS, XS = 8, 4


def joint_perm(step):
    pairs = []
    for dev in range(256):
        d, t = divmod(dev, 16)
        yh, z = divmod(d, ZS)
        yl, rest = divmod(t, 8)
        x, c = divmod(rest, 2)
        yh, z, yl, x, c = step(yh, z, yl, x, c)
        pairs.append((dev, (yh * ZS + z % ZS) * 16 + yl * 8 + (x % XS) * 2 + c))
    return pairs


SWAP_CORE = joint_perm(lambda yh, z, yl, x, c: (yh, z, yl, x, 1 - c))
SWAP_YL = joint_perm(lambda yh, z, yl, x, c: (yh, z, 1 - yl, x, c))
SWAP_YH = joint_perm(lambda yh, z, yl, x, c: (1 - yh, z, yl, x, c))
RING_X = joint_perm(lambda yh, z, yl, x, c: (yh, z, yl, x + 1 - 2 * c, c))
BACK_X = joint_perm(lambda yh, z, yl, x, c: (yh, z, yl, x - 1 + 2 * c, c))
BACK_Z = joint_perm(lambda yh, z, yl, x, c: (yh, z - 1 + 2 * c, yl, x, c))
RING_Z = joint_perm(lambda yh, z, yl, x, c: (yh, z + 1 - 2 * c, yl, x, c))


def permute(values, pairs):
    return lax.ppermute(values, BOTH, pairs)


def contract_trailing(left_side, right_side):
    return lax.dot_general(
        left_side, right_side, (((1,), (1,)), ((), ())), preferred_element_type=jnp.float32
    )


def gelu_parts(pre_values):
    normal_cdf = 0.5 * (1.0 + lax.erf(pre_values * 0.7071067811865476))
    density = jnp.exp(-0.5 * pre_values * pre_values) * 0.3989422804014327
    return (pre_values * normal_cdf, normal_cdf + pre_values * density)


def squares(values):
    return jnp.sum(values * values, axis=(1, 2))


def exchange(values, axis):
    return lax.all_to_all(values, axis, split_axis=0, concat_axis=0, tiled=True)


HALF_ROWS = 128


def nt(left_side, right_side):
    return contract_trailing(left_side, right_side)


def two_rows(value, columns):
    high = value.astype(jnp.bfloat16).astype(jnp.float32)
    row = lax.broadcasted_iota(jnp.int32, (16, columns), 0)
    rows = jnp.where(row == 0, high, jnp.where(row == 1, value - high, 0.0))
    return rows.astype(jnp.bfloat16)


def tn(left_side, right_side):
    return lax.dot_general(
        left_side, right_side, (((0,), (0,)), ((), ())), preferred_element_type=jnp.float32
    )


def product_kernel(sources, first, *refs):
    n = len(sources)
    arrays = 1 + max(part[0] for image in sources for part in image)
    images, cols, core = refs[:3]
    held, downs = refs[3 : 3 + arrays], refs[3 + arrays : 19 + arrays]
    slope, hidden, first_adapter, second_adapter = refs[19 + arrays : 23 + arrays]
    refs = refs[23 + arrays :]
    if not first:
        send_before = refs[1]
        refs = refs[4:]
    grad, send, b1_out, a2_out = refs[:4]
    cot_v, down_v, slope_v, hidden_v, grad_v, each_v, even, odd = refs[4:12]
    cot_sem, down_sem, slope_sem, hidden_sem, grad_sem, each_sem = refs[12:]
    feats = down_v.shape[1]
    block = feats // 16
    slots = cot_v.shape[0]

    def down_copy(k):
        at = pl.ds(pl.multiple_of(cols[k] * block, block), block)
        return pltpu.make_async_copy(downs[k], down_v.at[:, at], down_sem.at[k])

    def place(i):
        return pl.ds(pl.multiple_of(images[i] * PATCHES, PATCHES), PATCHES)

    def copies_in(i):
        slot = i % slots
        found = []
        for h in range(2):
            array, whose = sources[i][h]
            half = core[0] if whose == 1 else 1 - core[0]
            at = pl.ds(pl.multiple_of(half * HALF_ROWS, HALF_ROWS), HALF_ROWS)
            found.append(pltpu.make_async_copy(held[array], cot_v.at[slot, at], cot_sem.at[slot, h]))
        found.append(pltpu.make_async_copy(slope.at[place(i)], slope_v.at[slot], slope_sem.at[slot]))
        found.append(pltpu.make_async_copy(hidden.at[place(i)], hidden_v.at[slot], hidden_sem.at[slot]))
        return found

    def grad_copy(i):
        return pltpu.make_async_copy(grad_v.at[lax.rem(i, 2)], grad.at[place(i)], grad_sem.at[lax.rem(i, 2)])

    def each_copy(i, which):
        slot, to = lax.rem(i, 2), (b1_out, a2_out)[which]
        return pltpu.make_async_copy(each_v.at[slot, which], to.at[images[i]], each_sem.at[slot, which])

    def outgoing(i):
        return [grad_copy(i), each_copy(i, 0), each_copy(i, 1)]

    for copy in copies_in(0):
        copy.start()
    for k in range(16):
        down_copy(k).start()
    for i in range(1, slots - 1):
        for copy in copies_in(i):
            copy.start()
    send[...] = jnp.zeros_like(send) if first else send_before[...]
    for k in range(16):
        down_copy(k).wait()

    def arrive(i):
        slot = lax.rem(i, slots)
        for k in range(slots - 1, n):

            @pl.when(i + 1 == k)
            def _():
                for copy in copies_in(k):
                    copy.start()

        for h in range(2):
            landing = cot_v.at[slot, pl.ds(h * HALF_ROWS, HALF_ROWS)]
            pltpu.make_async_copy(landing, landing, cot_sem.at[slot, h]).wait()
        pltpu.make_async_copy(slope_v.at[slot], slope_v.at[slot], slope_sem.at[slot]).wait()
        pltpu.make_async_copy(hidden_v.at[slot], hidden_v.at[slot], hidden_sem.at[slot]).wait()
        return slot

    def finish(i, total):
        slot, way = lax.rem(i, slots), lax.rem(i, 2)
        image = images[i]
        rank_rows = cot_v[slot, :, feats:]
        adapter = jnp.dot(rank_rows[:, :32], first_adapter[...], preferred_element_type=jnp.float32)
        out = ((total[...] + adapter) * slope_v[slot]).astype(jnp.bfloat16)
        grad_v[way] = out
        rank = nt(second_adapter[...], out)
        b1 = tn(rank_rows[:, 32:64], out)
        a2 = tn(rank_rows[:, :32], hidden_v[slot])
        each_v[way, 0] = b1
        each_v[way, 1] = a2
        norm = two_rows(jnp.sum(b1 * b1 + a2 * a2, keepdims=True), HALF_ROWS)
        for to in range(2):
            send[2 * image + to, 0:32] = rank[:, :HALF_ROWS].astype(jnp.bfloat16)
            send[2 * image + to, 32:64] = rank[:, HALF_ROWS:].astype(jnp.bfloat16)
            send[2 * image + to, 64:80] = norm

    def drain(i):
        @pl.when(i > 1)
        def _():
            for copy in outgoing(i - 2):
                copy.wait()

    def step(i, now, before):
        slot = arrive(i)
        drain(i - 1)
        now[...] = nt(cot_v[slot, :, :feats], down_v[...])
        finish(i - 1, before)
        for copy in outgoing(i - 1):
            copy.start()

    slot = arrive(0)
    even[...] = nt(cot_v[slot, :, :feats], down_v[...])

    @pl.loop(1, n)
    def _(i):
        @pl.when(lax.rem(i, 2) == 1)
        def _():
            step(i, odd, even)

        @pl.when(lax.rem(i, 2) == 0)
        def _():
            step(i, even, odd)

    drain(n - 1)
    finish(n - 1, odd if n % 2 == 0 else even)
    for copy in outgoing(n - 1):
        copy.start()
    for copy in outgoing(n - 2) + outgoing(n - 1):
        copy.wait()


def product(sources, images, cols, core, held, downs, slope, hidden, adapters, before=None):
    n = len(sources)
    slots = 3
    group_rows, width = slope.shape
    feats = 16 * downs[0].shape[1]
    vmem = pl.BlockSpec(memory_space=pltpu.VMEM)
    smem = pl.BlockSpec(memory_space=pltpu.SMEM)
    hbm = pl.BlockSpec(memory_space=pl.ANY)
    stay = [pltpu.with_memory_space_constraint(v, pltpu.HBM) for v in (*held, *downs, slope, hidden)]
    operands = [images, cols, core, *stay, *adapters]
    specs = [smem] * 3 + [hbm] * len(stay) + [vmem] * 2
    each = pltpu.HBM((8, 32, width), jnp.float32)
    aliases = {}
    if before is not None:
        aliases = {len(operands) + k: k for k in (0, 2, 3)}
        operands += list(before)
        specs += [hbm, vmem, hbm, hbm]
    return pl.pallas_call(
        functools.partial(product_kernel, sources, before is None),
        out_shape=(
            jax.ShapeDtypeStruct((group_rows, width), jnp.bfloat16),
            jax.ShapeDtypeStruct((16, 80, HALF_ROWS), jnp.bfloat16),
            each,
            each,
        ),
        in_specs=specs,
        out_specs=(hbm, vmem, hbm, hbm),
        scratch_shapes=[
            pltpu.VMEM((slots, PATCHES, feats + HALF_ROWS), jnp.bfloat16),
            pltpu.VMEM((width, feats), jnp.bfloat16),
            pltpu.VMEM((slots, PATCHES, width), jnp.float32),
            pltpu.VMEM((slots, PATCHES, width), jnp.bfloat16),
            pltpu.VMEM((2, PATCHES, width), jnp.bfloat16),
            pltpu.VMEM((2, 2, 32, width), jnp.float32),
            pltpu.VMEM((PATCHES, width), jnp.float32),
            pltpu.VMEM((PATCHES, width), jnp.float32),
            pltpu.SemaphoreType.DMA((slots, 2)),
            pltpu.SemaphoreType.DMA((16,)),
            pltpu.SemaphoreType.DMA((slots,)),
            pltpu.SemaphoreType.DMA((slots,)),
            pltpu.SemaphoreType.DMA((2,)),
            pltpu.SemaphoreType.DMA((2, 2)),
        ],
        input_output_aliases=aliases,
        compiler_params=pltpu.CompilerParams(vmem_limit_bytes=40 * 2**20),
        cost_estimate=pl.CostEstimate(
            flops=2 * n * PATCHES * width * feats,
            bytes_accessed=2 * (n * PATCHES + width) * feats,
            transcendentals=0,
        ),
    )(*operands)


def in_vmem(kernel, out_shape, small, large=()):
    count, wide = len(small), len(large)

    def body(*refs):
        out, landed, sems = refs[count + wide], refs[count + wide + 1 : -1], refs[-1]
        copies = [
            pltpu.make_async_copy(refs[count + k], landed[k], sems.at[k]) for k in range(wide)
        ]
        for copy in copies:
            copy.start()
        for copy in copies:
            copy.wait()
        kernel(*refs[:count], *landed, out)

    specs = [
        pl.BlockSpec(memory_space=pltpu.SMEM if v.dtype == jnp.int32 else pltpu.VMEM) for v in small
    ]
    return pl.pallas_call(
        body,
        out_shape=out_shape,
        in_specs=specs + [pl.BlockSpec(memory_space=pl.ANY)] * wide,
        out_specs=pl.BlockSpec(memory_space=pltpu.VMEM),
        scratch_shapes=[pltpu.VMEM(v.shape, v.dtype) for v in large]
        + [pltpu.SemaphoreType.DMA((max(wide, 1),))],
        compiler_params=pltpu.CompilerParams(vmem_limit_bytes=20 * 2**20),
    )(*small, *(pltpu.with_memory_space_constraint(v, pltpu.HBM) for v in large))


def own_image(c, rank_0, rank_1, own_rows, sibling_rows):
    near = jnp.where(c == 0, rank_0, rank_1).astype(jnp.bfloat16)
    far = jnp.where(c == 0, rank_1, rank_0).astype(jnp.bfloat16)
    return jnp.dot(near, own_rows, preferred_element_type=jnp.float32) + jnp.dot(
        far, sibling_rows, preferred_element_type=jnp.float32
    )


def rank_kernel(cot_adapter, patch_adapter, cotangent, patches, out):
    ranks = [nt(cotangent[...], cot_adapter[...]), nt(patches[...], patch_adapter[...])]
    ranks.append(jnp.zeros((cotangent.shape[0], 64), jnp.float32))
    feats = cotangent.shape[1]
    out[:, :feats] = cotangent[...]
    out[:, feats:] = jnp.concatenate(ranks, axis=1).astype(jnp.bfloat16)


def b2_kernel(near, far, own_rows, sibling_rows, out):
    out[...] = jnp.dot(near[...], own_rows[...], preferred_element_type=jnp.float32) + jnp.dot(
        far[...], sibling_rows[:, : out.shape[1]], preferred_element_type=jnp.float32
    )


def clip_kernel(clip_norm, core, got, b2, own_rows, sibling_rows, out):
    c = core[0]
    total = got[0].astype(jnp.float32)
    for k in range(1, 16):
        total = total + got[k].astype(jnp.float32)
    a1 = own_image(c, total[:32], total[32:64], own_rows[...], sibling_rows[...])
    norm_sq = total[64:65, 0:1] + total[65:66, 0:1] + jnp.sum(a1 * a1, keepdims=True)
    norm_sq = norm_sq + jnp.sum(b2[...] * b2[...], keepdims=True)
    factor = jnp.minimum(1.0, clip_norm / jnp.sqrt(norm_sq + norm_eps))
    scale = two_rows(factor, 256)
    a1_half = jnp.where(c == 0, a1[:16], a1[16:]) * factor
    b2_half = jnp.where(c == 0, b2[:16], b2[16:]) * factor
    for k in range(16):
        out[k, 0:16] = a1_half[:, k * 256 : (k + 1) * 256].astype(jnp.bfloat16)
        out[k, 16:32] = b2_half[:, k * 256 : (k + 1) * 256].astype(jnp.bfloat16)
        out[k, 32:48] = scale


def weigh_kernel(got, b1, a2, out):
    for k in range(2):
        for which in range(2):
            rows = slice(16 * which, 16 * which + 16)
            halves = []
            for core in range(2):
                part = got[core, rows].astype(jnp.float32)
                for image in range(1, 8):
                    part = part + got[2 * image + core, rows].astype(jnp.float32)
                halves.append(part[:, k * 128 : (k + 1) * 128].astype(jnp.bfloat16))
            out[2 * which + k, 0:16] = halves[0]
            out[2 * which + k, 16:32] = halves[1]
    factors = []
    for image in range(8):
        rows = got[2 * image, 32:48].astype(jnp.float32)
        factors.append(rows[0:1, 0:1] + rows[1:2, 0:1])
    for which, each in enumerate((b1, a2)):
        for k in range(6):
            cols = slice(k * 128, (k + 1) * 128)
            part = factors[0] * each[0, :, cols]
            for image in range(1, 8):
                part = part + factors[image] * each[image, :, cols]
            out[4 + 6 * which + k] = part.astype(jnp.bfloat16)


def sum_kernel(got, out):
    total = got[0].astype(jnp.float32)
    for k in range(1, 16):
        total = total + got[k].astype(jnp.float32)
    for k in range(16):
        out[k] = total


def place_kernel(got, a1, b2, b1, a2):
    piece = 0
    for out in (a1, b2, b1, a2):
        for k in range(out.shape[1] // 128):
            out[:, k * 128 : (k + 1) * 128] = got[piece]
            piece += 1


def on_device(
    patches,
    cotangent,
    preact,
    down_matrix,
    up_adapter_first,
    up_adapter_second,
    down_adapter_first,
    down_adapter_second,
):
    rank_length = up_adapter_second.shape[0]
    hidden_width = preact.shape[1]
    feat_width = patches.shape[1]
    t, d = lax.axis_index("tensor"), lax.axis_index("dp")
    yl, x, c = t // 8, (t // 2) % XS, t % 2
    yh, z = d // ZS, d % ZS
    sign = 1 - 2 * c
    core = c.astype(jnp.int32)[None]
    clip_norm = clip_scale * math.sqrt(2.0 * rank_length * (feat_width + hidden_width * 16))

    kept, last = {}, None

    def received(name, value):
        nonlocal last
        if last is not None:
            value, kept[last] = lax.optimization_barrier((value, kept[last]))
        kept[name], last = value, name
        return value

    def after(value):
        value, kept[last] = lax.optimization_barrier((value, kept[last]))
        return value

    def swapped(value):
        return permute(value, SWAP_CORE)

    flying = {"E0": permute(down_matrix, SWAP_YH), "D1": permute(down_matrix, RING_Z)}
    def swap(name):
        flying["s" + name] = swapped(after(kept[name]))

    own_rows = in_vmem(
        rank_kernel,
        jax.ShapeDtypeStruct((cotangent.shape[0], feat_width + HALF_ROWS), jnp.bfloat16),
        (),
        (down_adapter_second, up_adapter_first, cotangent, patches),
    )
    kept["A0"], last = own_rows, "A0"
    flying["A1"], flying["A3"] = permute(own_rows, RING_X), permute(own_rows, BACK_X)
    onward = {
        "A1": [("A2", RING_X)],
        "A2": [("B2", SWAP_YL)],
        "B0": [("B1", RING_X), ("B3", BACK_X)],
    }

    def land(name):
        held = received(name, flying.pop(name))
        series, number = name[0], name[1:]
        if series in "DE" and int(number) < ZS - (1 if series == "D" else 2):
            flying[f"{series}{int(number) + 1}"] = permute(held, RING_Z)
        for to, pairs in onward.get(name, ()):
            flying[to] = permute(held, pairs)

    land("D1")
    land("E0")
    flying["B0"] = permute(after(own_rows), SWAP_YL)
    activation, gelu_slope = gelu_parts(after(preact).astype(jnp.float32))
    hidden_state = activation.astype(jnp.bfloat16)
    received("hidden", hidden_state)
    land("D2")
    land("E1")
    hidden_parts = contract_trailing(down_adapter_first, kept["hidden"])
    hidden_parts = hidden_parts.reshape(rank_length, 16, HALF_ROWS).transpose(1, 0, 2)
    high = lax.reduce_precision(hidden_parts, 8, 7)
    early = jnp.concatenate(
        [high.astype(jnp.bfloat16), (hidden_parts - high).astype(jnp.bfloat16)], axis=1
    )
    received("early", early)
    for name in ("D3", "E2", "A1", "A3", "D4", "E3", "B0", "A2", "D5", "E4", "D6", "E5", "D7"):
        land(name)
    flying["E7"] = permute(after(kept["E0"]), BACK_Z)
    for name in ("B1", "B3", "B2", "E6"):
        land(name)
    for j in range(XS):
        swap(f"A{j}")
    land("E7")
    for j in range(XS):
        swap(f"B{j}")
    got = exchange(kept["early"], "tensor")

    downs = [down_matrix] + [kept[f"D{j}"] for j in range(1, ZS)] + [kept[f"E{j}"] for j in range(ZS)]
    cols = [y * ZS + (z - sign * j) % ZS for y in (yh, 1 - yh) for j in range(ZS)]
    cols = jnp.stack(cols).astype(jnp.int32)

    def sibling(name):
        return kept[name] if name in kept else flying[name]

    held, sources, images = [], [], []
    for series, y_of in (("A", yl), ("B", 1 - yl)):
        for j in range(XS):
            sources.append(((len(held), 1), (len(held) + 1, -1)))
            held += [kept[f"{series}{j}"], sibling(f"s{series}{-j % XS}")]
            images.append(y_of * XS + (x - sign * j) % XS)
    patches_sib = swapped(after(patches))
    preact_gradient, to_owners, grad_b1_each, grad_a2_each = product(
        sources,
        jnp.stack(images).astype(jnp.int32),
        cols,
        core,
        held,
        downs,
        gelu_slope,
        kept["hidden"],
        (down_adapter_first, up_adapter_second),
    )
    got, to_owners = lax.optimization_barrier((got, to_owners))
    summed = jnp.sum(got.astype(jnp.float32), axis=0)
    hidden_rank = (summed[:rank_length] + summed[rank_length:]).astype(jnp.bfloat16)
    grad_b2_own = in_vmem(
        b2_kernel,
        jax.ShapeDtypeStruct((rank_length, feat_width), jnp.float32),
        (hidden_rank, swapped(hidden_rank)),
        (cotangent, flying["sA0"]),
    )

    clipped = in_vmem(
        functools.partial(clip_kernel, clip_norm),
        jax.ShapeDtypeStruct((16, 48, 256), jnp.bfloat16),
        (core, exchange(to_owners, "tensor"), grad_b2_own),
        (patches, patches_sib),
    )
    group_sums = in_vmem(
        weigh_kernel,
        jax.ShapeDtypeStruct((16, rank_length, 128), jnp.bfloat16),
        (exchange(clipped, "tensor"),),
        (grad_b1_each, grad_a2_each),
    )
    grads = in_vmem(
        sum_kernel,
        jax.ShapeDtypeStruct((16, rank_length, 128), jnp.float32),
        (exchange(group_sums, "dp"),),
    )
    widths = (feat_width // 16, feat_width // 16, hidden_width, hidden_width)
    vmem = pl.BlockSpec(memory_space=pltpu.VMEM)
    grad_a1, grad_b2, grad_b1, grad_a2 = pl.pallas_call(
        place_kernel,
        out_shape=tuple(jax.ShapeDtypeStruct((rank_length, w), jnp.float32) for w in widths),
        in_specs=[vmem],
        out_specs=(vmem,) * 4,
    )(exchange(grads, "dp"))
    return (preact_gradient, grad_a1, grad_b1, grad_a2, grad_b2)


def solution(mesh):
    placed = (
        P(("dp", "tensor"), None),
        P(("dp", "tensor"), None),
        P("dp", "tensor"),
        P("tensor", "dp"),
        P(),
        P(None, "tensor"),
        P(None, "tensor"),
        P(),
    )
    return jax.shard_map(
        on_device,
        mesh=mesh,
        in_specs=placed,
        out_specs=(
            P("dp", "tensor"),
            P(None, "tensor"),
            P(None, "tensor"),
            P(None, "tensor"),
            P(None, "tensor"),
        ),
        check_vma=False,
    )
```
